32 devices in a mesh: ex: 8 (over z, x), tp: 4 (over y, core).
Axes of the slice: x: 2, y: 2, z: 4, core: 2. Of those that a mesh axis runs over, the one named last changes fastest.
Arguments:
- activations: bfloat16 [32, 128, 8192], P('ex', None, 'tp'), may hold values from -6 to 6
- out_grads: bfloat16 [32, 128, 8192], P('ex', None, 'tp'), may hold values from -0.5390625 to 0.5390625
Outputs:
- fisher: float32 [8192, 8192], P('ex', 'tp')
The draws below stay inside these ranges and needn't reach their ends.
All inputs are finite; a program needn't handle non-finite values.
Results may differ from the reference program's by a relative error of at most 0.0003.
Values may be sent and summed in bfloat16 or wider, within the bound.
A program may use at most 128 MiB of HBM per device.

```python
import jax
import jax.numpy as jnp
from jax import lax

D = 8192
TOK = 128
EXAMPLES = 32


def spiked(entries, stream_key, source, target, shards_of, factor):
    def block_of(axis_at):
        return (jnp.arange(entries.shape[axis_at]) // (entries.shape[axis_at] // shards_of)).reshape((-1,) + (1,) * (entries.ndim - 1 - axis_at))

    one_side = jax.random.permutation(stream_key, shards_of)[block_of(target)]
    far = (block_of(target) + shards_of // 2) % shards_of
    return jnp.where((block_of(source) == one_side) | (block_of(source) == far), factor * entries, entries)


def block_levels(rng, shape, cuts, low, largest):
    loudness = 1.0
    for position, parts in cuts:
        draws = jax.random.uniform(jax.random.fold_in(jax.random.fold_in(rng, 6), position), (parts,), jnp.float32, low / len(cuts), largest / len(cuts))
        loudness = loudness * jnp.repeat(jnp.exp(draws), shape[position] // parts).reshape((-1,) + (1,) * (len(shape) - 1 - position))
    return loudness


def gaussian(stream_key, dims, scale, reach, cuts=(), dtype=jnp.bfloat16):
    result = jax.random.normal(stream_key, dims, jnp.float32) * scale
    if len(cuts) > 0:
        result = block_levels(stream_key, dims, cuts, -0.22, 0.18) * result
    return jnp.clip(result, min=-reach, max=reach).astype(dtype)


def heavy_noise(rng, extent, deviation, most, cuts, heavy, held_as=jnp.bfloat16):
    drawn = deviation * jax.random.normal(rng, extent, jnp.float32)
    if cuts:
        drawn = drawn * block_levels(rng, extent, cuts, -0.22, 0.18)
    return jnp.clip(spiked(drawn, jax.random.fold_in(rng, 3), *heavy), -most, most).astype(held_as)


def setup_inputs(seed: int = 0) -> dict:
    keys = jax.random.split(jax.random.key(seed), 3)
    return {
        "activations": heavy_noise(keys[0], (EXAMPLES, TOK, D), 1.0, 6.0, ((0, 8), (2, 4)), (0, 2, 8, 2.0)),
        "out_grads": gaussian(keys[1], (EXAMPLES, TOK, D), 0.09, 0.5390625, ((0, 8), (2, 4))),
    }


def reference(activations, out_grads):
    def add_example(running, pair):
        inputs_rows, grads_rows = pair
        gradient = jnp.dot(inputs_rows.T, grads_rows, preferred_element_type=jnp.float32)
        return running + gradient * gradient, None

    start_value = jnp.zeros((activations.shape[2], out_grads.shape[2]), jnp.float32)
    fisher, unused = lax.scan(add_example, start_value, (activations, out_grads))
    return fisher
```

```python
import functools

import jax
import jax.numpy as jnp
from jax import lax
from jax.experimental import pallas as pl
from jax.experimental.pallas import tpu as pltpu
from jax.sharding import PartitionSpec as P

MESH = pl.DeviceIdType.MESH
LINE = 4
BY_LINE = 1
CORES = 2


def tile_of(size, most):
    while size % most:
        most //= 2
    return most


def kernel(n_ex, n_tp, act_ref, og_ref, out_ref, acts, ogs, acc, lhs,
           own_sem, og_recv, up_send, down_send, across_send,
           part_send, part_recv, y_send, sib_send, share_recv, out_sem):
    examples, tokens, width = og_ref.shape
    rows = acc.shape[0]
    line, wide = LINE, n_ex // LINE
    per_owner = width // rows
    ys = n_tp // CORES
    quarter = act_ref.shape[0] // n_tp

    me, tp = lax.axis_index("ex"), lax.axis_index("tp")
    z, x = me // wide, lax.rem(me, wide)
    y, core = tp // CORES, lax.rem(tp, CORES)
    owner = me // per_owner
    mine = owner == tp

    def chunk(zz, xx, k):
        return (zz * wide + xx) * examples + k

    def other(first, step, size):
        return lax.rem(first + step, size)

    barrier = pltpu.get_barrier_semaphore()

    def greet(ex, t):
        pl.semaphore_signal(barrier, inc=1, device_id={"ex": ex, "tp": t}, device_id_type=MESH)

    @pl.when(z > 0)
    def _():
        greet(me - wide, tp)

    @pl.when(z < line - 1)
    def _():
        greet(me + wide, tp)

    for d in range(1, wide):
        greet(z * wide + other(x, d, wide), tp)
    for d in range(1, ys):
        greet(me, other(y, d, ys) * CORES + core)
    greet(me, y * CORES + 1 - core)

    @pl.loop(0, n_ex)
    def _(ex):
        @pl.when(jnp.logical_not(jnp.logical_and(ex == me, mine)))
        def _():
            greet(ex, owner)

    count = (z > 0).astype(jnp.int32) + (z < line - 1).astype(jnp.int32) - mine.astype(jnp.int32)
    pl.semaphore_wait(barrier, count + (wide - 1) + (ys - 1) + 1 + per_owner * n_tp)

    def part(j, t):
        return pltpu.make_async_remote_copy(
            src_ref=act_ref.at[pl.ds(t * quarter, quarter), pl.ds(j * rows, rows)],
            dst_ref=acts.at[me, pl.ds(t * quarter, quarter)],
            send_sem=part_send.at[j * n_tp + t], recv_sem=part_recv.at[me],
            device_id={"ex": tp * per_owner + j, "tp": t}, device_id_type=MESH)

    def own_part(j):
        return pltpu.make_async_copy(
            act_ref.at[pl.ds(tp * quarter, quarter), pl.ds(j * rows, rows)],
            acts.at[me, pl.ds(tp * quarter, quarter)], part_recv.at[me])

    def piece(ex, t):
        return acts.at[ex, pl.ds(t * quarter, quarter)]

    def share_y(ex, d):
        return pltpu.make_async_remote_copy(
            src_ref=piece(ex, tp), dst_ref=piece(ex, tp),
            send_sem=y_send.at[ex * ys + d], recv_sem=share_recv.at[ex * n_tp + tp],
            device_id={"ex": me, "tp": other(y, d, ys) * CORES + core}, device_id_type=MESH)

    def share_core(ex, yy):
        t = yy * CORES + core
        return pltpu.make_async_remote_copy(
            src_ref=piece(ex, t), dst_ref=piece(ex, t),
            send_sem=sib_send.at[ex * ys + yy], recv_sem=share_recv.at[ex * n_tp + t],
            device_id={"ex": me, "tp": y * CORES + 1 - core}, device_id_type=MESH)

    def arrived(ref, sem):
        pltpu.make_async_copy(ref, ref, sem).wait()

    def og_copy(c, source, sems, slot, ex):
        return pltpu.make_async_remote_copy(
            src_ref=source, dst_ref=ogs.at[c], send_sem=sems.at[slot], recv_sem=og_recv.at[c],
            device_id={"ex": ex, "tp": tp}, device_id_type=MESH)

    def up(c, source):
        return og_copy(c, source, up_send, c, me + wide)

    def down(c, source):
        return og_copy(c, source, down_send, c, me - wide)

    def across(c, source, d):
        return og_copy(c, source, across_send, c * wide + d, z * wide + other(x, d, wide))

    def own_load():
        return pltpu.make_async_copy(og_ref, ogs.at[pl.ds(me * examples, examples)], own_sem)

    def each_part(act):
        @pl.loop(0, per_owner * n_tp)
        def _(i):
            j, t = i // n_tp, lax.rem(i, n_tp)
            itself = jnp.logical_and(tp * per_owner + j == me, t == tp)
            act(j, t, itself)

    def start_part(j, t, itself):
        @pl.when(itself)
        def _():
            own_part(j).start()

        @pl.when(jnp.logical_not(itself))
        def _():
            part(j, t).start()

    def end_part(j, t, itself):
        @pl.when(jnp.logical_not(itself))
        def _():
            part(j, t).wait_send()

    def own_copies(go):
        @pl.loop(0, examples)
        def _(k):
            c = chunk(z, x, k)
            for d in range(1, wide):
                go(across(c, og_ref.at[k], d))

            @pl.when(z < line - 1)
            def _():
                go(up(c, og_ref.at[k]))

            @pl.when(z > 0)
            def _():
                go(down(c, og_ref.at[k]))

    def line_copies(go, ready, s):
        @pl.loop(0, examples)
        def _(k):
            for step in (-1, 1):
                zz = z + step * s

                @pl.when(jnp.logical_and(zz >= 0, zz < line))
                def _():
                    c = chunk(zz, x, k)
                    ready(c)
                    if step < 0:
                        @pl.when(z < line - 1)
                        def _():
                            go(up(c, ogs.at[c]))
                    else:
                        @pl.when(z > 0)
                        def _():
                            go(down(c, ogs.at[c]))

                    @pl.when(jnp.logical_or(s > 1, k >= BY_LINE))
                    def _():
                        for d in range(1, wide):
                            go(across(c, ogs.at[c], d))

    def side_copies(go, ready):
        for k in range(BY_LINE):
            for d in range(1, wide):
                c = chunk(z, other(x, d, wide), k)
                ready(c)

                @pl.when(z < line - 1)
                def _():
                    go(up(c, ogs.at[c]))

                @pl.when(z > 0)
                def _():
                    go(down(c, ogs.at[c]))

    def start(copy):
        copy.start()

    def sent(copy):
        copy.wait_send()

    def og_ready(c):
        arrived(ogs.at[c], og_recv.at[c])

    def nothing(c):
        pass

    def act_parts(first, last):
        @pl.loop(first, last)
        def _(i):
            ex = lax.rem(me + i, n_ex)
            arrived(piece(ex, tp), part_recv.at[ex])
            for d in range(1, ys):
                share_y(ex, d).start()
            share_core(ex, y).start()

    def act_shares():
        @pl.loop(0, n_ex)
        def _(i):
            ex = lax.rem(me + i, n_ex)
            for d in range(1, ys):
                yy = other(y, d, ys)
                t = yy * CORES + core
                arrived(piece(ex, t), share_recv.at[ex * n_tp + t])
                share_core(ex, yy).start()

    each_part(start_part)
    own_copies(start)
    own_load().start()
    acc[...] = jnp.zeros_like(acc)
    line_copies(start, og_ready, 1)
    side_copies(start, og_ready)
    act_parts(0, n_ex // 2)
    for s in range(2, line):
        line_copies(start, og_ready, s)
        if s == 2:
            act_parts(n_ex // 2, n_ex)
    act_shares()
    own_load().wait()

    row_tile, col_tile = tile_of(rows, 256), tile_of(width, 512)

    def add_source(ex):
        @pl.loop(0, rows // row_tile)
        def _(i):
            r = pl.ds(pl.multiple_of(i * row_tile, row_tile), row_tile)
            for k in range(examples):
                lhs[k] = acts[ex, pl.ds(k * tokens, tokens), r].T

            @pl.loop(0, width // col_tile)
            def _(j):
                q = pl.ds(pl.multiple_of(j * col_tile, col_tile), col_tile)
                total = acc[r, q]
                for k in range(examples):
                    g = jnp.dot(lhs[k], ogs[ex * examples + k, :, q], preferred_element_type=jnp.float32)
                    total = total + g * g
                acc[r, q] = total

    spread = 2 * line - 1

    @pl.loop(0, wide * spread)
    def _(i):
        d, v = i // spread, lax.rem(i, spread)
        zz = z + ((v + 1) // 2) * (2 * lax.rem(v, 2) - 1)

        @pl.when(jnp.logical_and(zz >= 0, zz < line))
        def _():
            xx = other(x, d, wide)
            ex = zz * wide + xx
            for yy in range(ys):
                t = yy * CORES + 1 - core
                arrived(piece(ex, t), share_recv.at[ex * n_tp + t])

            @pl.when(d > 0)
            def _():
                @pl.loop(0, examples)
                def _(k):
                    @pl.when(jnp.logical_or(zz != z, k >= BY_LINE))
                    def _():
                        og_ready(chunk(zz, xx, k))

            add_source(ex)

    result = pltpu.make_async_copy(acc, out_ref, out_sem)
    result.start()

    each_part(end_part)
    own_copies(sent)
    for s in range(1, line):
        line_copies(sent, nothing, s)
    side_copies(sent, nothing)

    @pl.loop(0, n_ex)
    def _(ex):
        for d in range(1, ys):
            share_y(ex, d).wait_send()
        for yy in range(ys):
            share_core(ex, yy).wait_send()

    result.wait()


def solution(mesh):
    n_ex, n_tp = mesh.shape["ex"], mesh.shape["tp"]

    def body(activations, out_grads):
        examples, tokens, width = out_grads.shape
        rows = width * n_tp // n_ex
        flat = activations.reshape(examples * tokens, width)
        chunks = n_ex * examples
        wide = n_ex // LINE
        ys = n_tp // CORES
        dma = pltpu.SemaphoreType.DMA
        return pl.pallas_call(
            functools.partial(kernel, n_ex, n_tp),
            out_shape=jax.ShapeDtypeStruct((rows, width), jnp.float32),
            in_specs=[pl.BlockSpec(memory_space=pl.ANY)] * 2,
            out_specs=pl.BlockSpec(memory_space=pl.ANY),
            scratch_shapes=[
                pltpu.VMEM((n_ex, examples * tokens, rows), jnp.bfloat16),
                pltpu.VMEM((chunks, tokens, width), jnp.bfloat16),
                pltpu.VMEM((rows, width), jnp.float32),
                pltpu.VMEM((examples, tile_of(rows, 256), tokens), jnp.bfloat16),
                dma,
                dma((chunks,)),
                dma((chunks,)),
                dma((chunks,)),
                dma((chunks * wide,)),
                dma((width // rows * n_tp,)),
                dma((n_ex,)),
                dma((n_ex * ys,)),
                dma((n_ex * ys,)),
                dma((n_ex * n_tp,)),
                dma,
            ],
            compiler_params=pltpu.CompilerParams(
                collective_id=0, has_side_effects=True, vmem_limit_bytes=48 * 1024 * 1024),
            cost_estimate=pl.CostEstimate(
                flops=2 * rows * width * chunks * tokens,
                bytes_accessed=12 * 1024 * 1024, transcendentals=0),
        )(flat, out_grads)

    return jax.shard_map(
        body,
        mesh=mesh,
        in_specs=(P("ex", None, "tp"), P("ex", None, "tp")),
        out_specs=P("ex", "tp"),
        check_vma=False,
    )
```

```python
import functools

import jax
import jax.numpy as jnp
from jax import lax
from jax.experimental import pallas as pl
from jax.experimental.pallas import tpu as pltpu
from jax.sharding import PartitionSpec as P

MESH = pl.DeviceIdType.MESH
LINE = 4
BY_LINE = 1
CORES = 2


def tile_of(size, most):
    while size % most:
        most //= 2
    return most


def kernel(n_ex, n_tp, act_ref, og_ref, out_ref, acts, ogs, lhs,
           own_sem, og_recv, up_send, down_send, across_send,
           part_send, part_recv, y_send, sib_send, share_recv):
    examples, tokens, width = og_ref.shape
    rows = out_ref.shape[0]
    line, wide = LINE, n_ex // LINE
    per_owner = width // rows
    ys = n_tp // CORES
    quarter = act_ref.shape[0] // n_tp

    me, tp = lax.axis_index("ex"), lax.axis_index("tp")
    z, x = me // wide, lax.rem(me, wide)
    y, core = tp // CORES, lax.rem(tp, CORES)
    owner = me // per_owner
    mine = owner == tp

    def chunk(zz, xx, k):
        return (zz * wide + xx) * examples + k

    def other(first, step, size):
        return lax.rem(first + step, size)

    barrier = pltpu.get_barrier_semaphore()

    def greet(ex, t):
        pl.semaphore_signal(barrier, inc=1, device_id={"ex": ex, "tp": t}, device_id_type=MESH)

    @pl.when(z > 0)
    def _():
        greet(me - wide, tp)

    @pl.when(z < line - 1)
    def _():
        greet(me + wide, tp)

    for d in range(1, wide):
        greet(z * wide + other(x, d, wide), tp)
    for d in range(1, ys):
        greet(me, other(y, d, ys) * CORES + core)
    greet(me, y * CORES + 1 - core)

    @pl.loop(0, n_ex)
    def _(ex):
        @pl.when(jnp.logical_not(jnp.logical_and(ex == me, mine)))
        def _():
            greet(ex, owner)

    count = (z > 0).astype(jnp.int32) + (z < line - 1).astype(jnp.int32) - mine.astype(jnp.int32)
    pl.semaphore_wait(barrier, count + (wide - 1) + (ys - 1) + 1 + per_owner * n_tp)

    def part(j, t):
        return pltpu.make_async_remote_copy(
            src_ref=act_ref.at[pl.ds(t * quarter, quarter), pl.ds(j * rows, rows)],
            dst_ref=acts.at[me, pl.ds(t * quarter, quarter)],
            send_sem=part_send.at[j * n_tp + t], recv_sem=part_recv.at[me],
            device_id={"ex": tp * per_owner + j, "tp": t}, device_id_type=MESH)

    def own_part(j):
        return pltpu.make_async_copy(
            act_ref.at[pl.ds(tp * quarter, quarter), pl.ds(j * rows, rows)],
            acts.at[me, pl.ds(tp * quarter, quarter)], part_recv.at[me])

    def piece(ex, t):
        return acts.at[ex, pl.ds(t * quarter, quarter)]

    def share_y(ex, d):
        return pltpu.make_async_remote_copy(
            src_ref=piece(ex, tp), dst_ref=piece(ex, tp),
            send_sem=y_send.at[ex * ys + d], recv_sem=share_recv.at[ex * n_tp + tp],
            device_id={"ex": me, "tp": other(y, d, ys) * CORES + core}, device_id_type=MESH)

    def share_core(ex, yy):
        t = yy * CORES + core
        return pltpu.make_async_remote_copy(
            src_ref=piece(ex, t), dst_ref=piece(ex, t),
            send_sem=sib_send.at[ex * ys + yy], recv_sem=share_recv.at[ex * n_tp + t],
            device_id={"ex": me, "tp": y * CORES + 1 - core}, device_id_type=MESH)

    def arrived(ref, sem):
        pltpu.make_async_copy(ref, ref, sem).wait()

    def og_copy(c, source, sems, slot, ex):
        return pltpu.make_async_remote_copy(
            src_ref=source, dst_ref=ogs.at[c], send_sem=sems.at[slot], recv_sem=og_recv.at[c],
            device_id={"ex": ex, "tp": tp}, device_id_type=MESH)

    def up(c, source):
        return og_copy(c, source, up_send, c, me + wide)

    def down(c, source):
        return og_copy(c, source, down_send, c, me - wide)

    def across(c, source, d):
        return og_copy(c, source, across_send, c * wide + d, z * wide + other(x, d, wide))

    def own_load():
        return pltpu.make_async_copy(og_ref, ogs.at[pl.ds(me * examples, examples)], own_sem)

    def each_part(act):
        @pl.loop(0, per_owner * n_tp)
        def _(i):
            j, t = i // n_tp, lax.rem(i, n_tp)
            itself = jnp.logical_and(tp * per_owner + j == me, t == tp)
            act(j, t, itself)

    def start_part(j, t, itself):
        @pl.when(itself)
        def _():
            own_part(j).start()

        @pl.when(jnp.logical_not(itself))
        def _():
            part(j, t).start()

    def end_part(j, t, itself):
        @pl.when(jnp.logical_not(itself))
        def _():
            part(j, t).wait_send()

    def own_copies(go):
        @pl.loop(0, examples)
        def _(k):
            c = chunk(z, x, k)
            for d in range(1, wide):
                go(across(c, og_ref.at[k], d))

            @pl.when(z < line - 1)
            def _():
                go(up(c, og_ref.at[k]))

            @pl.when(z > 0)
            def _():
                go(down(c, og_ref.at[k]))

    def line_step(go, ready, s, k):
        for step in (-1, 1):
            zz = z + step * s

            @pl.when(jnp.logical_and(zz >= 0, zz < line))
            def _():
                c = chunk(zz, x, k)
                ready(c)
                if step < 0:
                    @pl.when(z < line - 1)
                    def _():
                        go(up(c, ogs.at[c]))
                else:
                    @pl.when(z > 0)
                    def _():
                        go(down(c, ogs.at[c]))

                @pl.when(jnp.logical_or(s > 1, k >= BY_LINE))
                def _():
                    for d in range(1, wide):
                        go(across(c, ogs.at[c], d))

    def side_copies(go, ready):
        for k in range(BY_LINE):
            for d in range(1, wide):
                c = chunk(z, other(x, d, wide), k)
                ready(c)

                @pl.when(z < line - 1)
                def _():
                    go(up(c, ogs.at[c]))

                @pl.when(z > 0)
                def _():
                    go(down(c, ogs.at[c]))

    def start(copy):
        copy.start()

    def sent(copy):
        copy.wait_send()

    def og_ready(c):
        arrived(ogs.at[c], og_recv.at[c])

    def nothing(c):
        pass

    def act_source(i):
        far = i // wide
        below = jnp.minimum(z, line - 1 - z)
        near = jnp.where(lax.rem(far, 2) == 1, z - (far + 1) // 2, z + far // 2)
        end = jnp.where(z < line - 1 - z, far, line - 1 - far)
        zz = jnp.where(far <= 2 * below, near, end)
        return zz * wide + lax.rem(x + lax.rem(i, wide), wide)

    def act_parts(first, last):
        @pl.loop(first, last)
        def _(i):
            ex = act_source(i)
            arrived(piece(ex, tp), part_recv.at[ex])
            for d in range(1, ys):
                share_y(ex, d).start()
            share_core(ex, y).start()

    def act_shares(first, last):
        @pl.loop(first, last)
        def _(i):
            ex = act_source(i)
            for d in range(1, ys):
                yy = other(y, d, ys)
                t = yy * CORES + core
                arrived(piece(ex, t), share_recv.at[ex * n_tp + t])
                share_core(ex, yy).start()

    col_tile = tile_of(width, 512)

    def add_example(ex, k):
        lhs[...] = acts[ex, pl.ds(pl.multiple_of(k * tokens, tokens), tokens), :].T

        @pl.loop(0, width // col_tile)
        def _(j):
            q = pl.ds(pl.multiple_of(j * col_tile, col_tile), col_tile)
            g = jnp.dot(lhs[...], ogs[ex * examples + k, :, q], preferred_element_type=jnp.float32)
            out_ref[:, q] += g * g

    slots = wide + (line - 1) * 2 * wide

    def add_source(n):
        far = n >= wide
        m = jnp.maximum(n - wide, 0)
        s = jnp.where(far, 1 + m // (2 * wide), 0)
        d = jnp.where(far, lax.rem(m, 2 * wide) // 2, n)
        zz = z + s * (2 * lax.rem(m, 2) - 1)

        @pl.when(jnp.logical_and(zz >= 0, zz < line))
        def _():
            xx = lax.rem(x + d, wide)
            ex = zz * wide + xx
            for yy in range(ys):
                t = yy * CORES + 1 - core
                arrived(piece(ex, t), share_recv.at[ex * n_tp + t])

            @pl.loop(0, examples)
            def _(k):
                @pl.when(jnp.logical_and(d > 0, jnp.logical_or(zz != z, k >= BY_LINE)))
                def _():
                    og_ready(chunk(zz, xx, k))

                add_example(ex, k)

    each_part(start_part)
    own_copies(start)
    own_load().start()
    out_ref[...] = jnp.zeros_like(out_ref)
    own_load().wait()
    each = -(-n_ex // examples)
    more = -(-n_ex // (2 * examples))

    @pl.loop(0, examples + slots)
    def _(i):
        s, k = 1 + i // examples, lax.rem(i, examples)

        @pl.when(s < line)
        def _():
            line_step(start, og_ready, s, k)

        @pl.when(s == 1)
        def _():
            act_parts(k * each, jnp.minimum(k * each + each, n_ex))

        @pl.when(i == examples - 1)
        def _():
            side_copies(start, og_ready)
            act_shares(0, more)

        @pl.when(i >= examples)
        def _():
            @pl.when(s == 2)
            def _():
                first = more + k * each
                act_shares(jnp.minimum(first, n_ex), jnp.minimum(first + each, n_ex))

            add_source(i - examples)

    each_part(end_part)
    own_copies(sent)

    @pl.loop(0, (line - 1) * examples)
    def _(i):
        line_step(sent, nothing, 1 + i // examples, lax.rem(i, examples))

    side_copies(sent, nothing)

    @pl.loop(0, n_ex)
    def _(ex):
        for d in range(1, ys):
            share_y(ex, d).wait_send()
        for yy in range(ys):
            share_core(ex, yy).wait_send()


def solution(mesh):
    n_ex, n_tp = mesh.shape["ex"], mesh.shape["tp"]

    def body(activations, out_grads):
        examples, tokens, width = out_grads.shape
        rows = width * n_tp // n_ex
        flat = activations.reshape(examples * tokens, width)
        chunks = n_ex * examples
        wide = n_ex // LINE
        ys = n_tp // CORES
        dma = pltpu.SemaphoreType.DMA
        return pl.pallas_call(
            functools.partial(kernel, n_ex, n_tp),
            out_shape=jax.ShapeDtypeStruct((rows, width), jnp.float32),
            in_specs=[pl.BlockSpec(memory_space=pl.ANY)] * 2,
            out_specs=pl.BlockSpec(memory_space=pltpu.VMEM),
            scratch_shapes=[
                pltpu.VMEM((n_ex, examples * tokens, rows), jnp.bfloat16),
                pltpu.VMEM((chunks, tokens, width), jnp.bfloat16),
                pltpu.VMEM((rows, tokens), jnp.bfloat16),
                dma,
                dma((chunks,)),
                dma((chunks,)),
                dma((chunks,)),
                dma((chunks * wide,)),
                dma((width // rows * n_tp,)),
                dma((n_ex,)),
                dma((n_ex * ys,)),
                dma((n_ex * ys,)),
                dma((n_ex * n_tp,)),
            ],
            compiler_params=pltpu.CompilerParams(
                collective_id=0, has_side_effects=True, vmem_limit_bytes=40 * 1024 * 1024),
            cost_estimate=pl.CostEstimate(
                flops=2 * rows * width * chunks * tokens,
                bytes_accessed=12 * 1024 * 1024, transcendentals=0),
        )(flat, out_grads)

    return jax.shard_map(
        body,
        mesh=mesh,
        in_specs=(P("ex", None, "tp"), P("ex", None, "tp")),
        out_specs=P("ex", "tp"),
        check_vma=False,
    )
```

```python
import functools

import jax
import jax.numpy as jnp
from jax import lax
from jax.experimental import pallas as pl
from jax.experimental.pallas import tpu as pltpu
from jax.sharding import PartitionSpec as P

MESH = pl.DeviceIdType.MESH
LINE = 4
BY_LINE = 1
CORES = 2


def tile_of(size, most):
    while size % most:
        most //= 2
    return most


def kernel(n_ex, n_tp, act_ref, og_ref, out_ref, acts, ogs, relay, lhs,
           own_sem, og_recv, up_send, down_send, across_send,
           part_send, part_recv, relay_send, relay_recv, y_send, sib_send, share_recv):
    examples, tokens, width = og_ref.shape
    rows = out_ref.shape[0]
    line, wide = LINE, n_ex // LINE
    per_owner = width // rows
    ys = n_tp // CORES
    quarter = act_ref.shape[0] // n_tp

    me, tp = lax.axis_index("ex"), lax.axis_index("tp")
    z, x = me // wide, lax.rem(me, wide)
    y, core = tp // CORES, lax.rem(tp, CORES)
    owner = me // per_owner
    mine = lax.rem(owner, CORES) == core

    def chunk(zz, xx, k):
        return (zz * wide + xx) * examples + k

    def other(first, step, size):
        return lax.rem(first + step, size)

    barrier = pltpu.get_barrier_semaphore()

    def greet(ex, t):
        pl.semaphore_signal(barrier, inc=1, device_id={"ex": ex, "tp": t}, device_id_type=MESH)

    @pl.when(z > 0)
    def _():
        greet(me - wide, tp)

    @pl.when(z < line - 1)
    def _():
        greet(me + wide, tp)

    for d in range(1, wide):
        greet(z * wide + other(x, d, wide), tp)
    for d in range(1, ys):
        greet(me, other(y, d, ys) * CORES + core)
    greet(me, y * CORES + 1 - core)

    @pl.loop(0, n_ex)
    def _(ex):
        @pl.when(jnp.logical_not(jnp.logical_and(ex == me, mine)))
        def _():
            greet(ex, y * CORES + lax.rem(owner, CORES))

    count = (z > 0).astype(jnp.int32) + (z < line - 1).astype(jnp.int32) - mine.astype(jnp.int32)
    pl.semaphore_wait(barrier, count + (wide - 1) + (ys - 1) + 1 + per_owner * n_tp)

    def to_relay(d, c):
        to = other(y, d, ys)
        return pltpu.make_async_remote_copy(
            src_ref=act_ref.at[pl.ds((to * CORES + c) * quarter, quarter)], dst_ref=relay.at[y, c],
            send_sem=relay_send.at[d * CORES + c], recv_sem=relay_recv.at[y * CORES + c],
            device_id={"ex": me, "tp": to * CORES + core}, device_id_type=MESH)

    def part(source, from_y, c, j):
        t = y * CORES + c
        return pltpu.make_async_remote_copy(
            src_ref=source.at[:, pl.ds(j * rows, rows)],
            dst_ref=acts.at[me, pl.ds(t * quarter, quarter)],
            send_sem=part_send.at[(from_y * CORES + c) * per_owner + j], recv_sem=part_recv.at[me],
            device_id={"ex": (from_y * CORES + core) * per_owner + j, "tp": t}, device_id_type=MESH)

    def own_part(source, j):
        return pltpu.make_async_copy(
            source.at[:, pl.ds(j * rows, rows)],
            acts.at[me, pl.ds(tp * quarter, quarter)], part_recv.at[me])

    def parts_from(source, from_y, c, begin):
        for j in range(per_owner):
            itself = jnp.logical_and((from_y * CORES + core) * per_owner + j == me, c == core)

            @pl.when(jnp.logical_not(itself))
            def _():
                if begin:
                    part(source, from_y, c, j).start()
                else:
                    part(source, from_y, c, j).wait_send()

            if begin:
                @pl.when(itself)
                def _():
                    own_part(source, j).start()

    def direct_parts(begin):
        for c in range(CORES):
            parts_from(act_ref.at[pl.ds((y * CORES + c) * quarter, quarter)], y, c, begin)

    def relayed_parts(begin):
        for d in range(1, ys):
            from_y = other(y, d, ys)
            for c in range(CORES):
                if begin:
                    arrived(relay.at[from_y, c], relay_recv.at[from_y * CORES + c])
                parts_from(relay.at[from_y, c], from_y, c, begin)

    def relays(go):
        for d in range(1, ys):
            for c in range(CORES):
                go(to_relay(d, c))

    def piece(ex, t):
        return acts.at[ex, pl.ds(t * quarter, quarter)]

    def share_y(ex, d):
        return pltpu.make_async_remote_copy(
            src_ref=piece(ex, tp), dst_ref=piece(ex, tp),
            send_sem=y_send.at[ex * ys + d], recv_sem=share_recv.at[ex * n_tp + tp],
            device_id={"ex": me, "tp": other(y, d, ys) * CORES + core}, device_id_type=MESH)

    def share_core(ex, yy):
        t = yy * CORES + core
        return pltpu.make_async_remote_copy(
            src_ref=piece(ex, t), dst_ref=piece(ex, t),
            send_sem=sib_send.at[ex * ys + yy], recv_sem=share_recv.at[ex * n_tp + t],
            device_id={"ex": me, "tp": y * CORES + 1 - core}, device_id_type=MESH)

    def arrived(ref, sem):
        pltpu.make_async_copy(ref, ref, sem).wait()

    def og_copy(c, source, sems, slot, ex):
        return pltpu.make_async_remote_copy(
            src_ref=source, dst_ref=ogs.at[c], send_sem=sems.at[slot], recv_sem=og_recv.at[c],
            device_id={"ex": ex, "tp": tp}, device_id_type=MESH)

    def up(c, source):
        return og_copy(c, source, up_send, c, me + wide)

    def down(c, source):
        return og_copy(c, source, down_send, c, me - wide)

    def across(c, source, d):
        return og_copy(c, source, across_send, c * wide + d, z * wide + other(x, d, wide))

    def own_load():
        return pltpu.make_async_copy(og_ref, ogs.at[pl.ds(me * examples, examples)], own_sem)

    def own_copies(go, first, last):
        @pl.loop(first, last)
        def _(k):
            c = chunk(z, x, k)
            for d in range(1, wide):
                go(across(c, og_ref.at[k], d))

            @pl.when(z < line - 1)
            def _():
                go(up(c, og_ref.at[k]))

            @pl.when(z > 0)
            def _():
                go(down(c, og_ref.at[k]))

    def line_step(go, ready, s, k):
        for step in (-1, 1):
            zz = z + step * s

            @pl.when(jnp.logical_and(zz >= 0, zz < line))
            def _():
                c = chunk(zz, x, k)
                ready(c)
                if step < 0:
                    @pl.when(z < line - 1)
                    def _():
                        go(up(c, ogs.at[c]))
                else:
                    @pl.when(z > 0)
                    def _():
                        go(down(c, ogs.at[c]))

                @pl.when(jnp.logical_or(s > 1, k >= BY_LINE))
                def _():
                    for d in range(1, wide):
                        go(across(c, ogs.at[c], d))

    def side_copies(go, ready):
        for k in range(BY_LINE):
            for d in range(1, wide):
                c = chunk(z, other(x, d, wide), k)
                ready(c)

                @pl.when(z < line - 1)
                def _():
                    go(up(c, ogs.at[c]))

                @pl.when(z > 0)
                def _():
                    go(down(c, ogs.at[c]))

    def start(copy):
        copy.start()

    def sent(copy):
        copy.wait_send()

    def og_ready(c):
        arrived(ogs.at[c], og_recv.at[c])

    def nothing(c):
        pass

    slots = wide + (line - 1) * 2 * wide

    def at_slot(n, act):
        far = n >= wide
        m = jnp.maximum(n - wide, 0)
        s = jnp.where(far, 1 + m // (2 * wide), 0)
        d = jnp.where(far, lax.rem(m, 2 * wide) // 2, n)
        zz = z + s * (2 * lax.rem(m, 2) - 1)

        @pl.when(jnp.logical_and(jnp.logical_and(n >= 0, n < slots), jnp.logical_and(zz >= 0, zz < line)))
        def _():
            act(d, zz, lax.rem(x + d, wide))

    def act_parts(d, zz, xx):
        ex = zz * wide + xx
        arrived(piece(ex, tp), part_recv.at[ex])
        for e in range(1, ys):
            share_y(ex, e).start()
        share_core(ex, y).start()

    def act_shares(d, zz, xx):
        ex = zz * wide + xx
        for e in range(1, ys):
            yy = other(y, e, ys)
            t = yy * CORES + core
            arrived(piece(ex, t), share_recv.at[ex * n_tp + t])
            share_core(ex, yy).start()

    col_tile = tile_of(width, 512)

    def add_example(ex, k):
        lhs[...] = acts[ex, pl.ds(pl.multiple_of(k * tokens, tokens), tokens), :].T

        @pl.loop(0, width // col_tile)
        def _(j):
            q = pl.ds(pl.multiple_of(j * col_tile, col_tile), col_tile)
            g = jnp.dot(lhs[...], ogs[ex * examples + k, :, q], preferred_element_type=jnp.float32)
            out_ref[:, q] += g * g

    def add_source(d, zz, xx):
        ex = zz * wide + xx
        for yy in range(ys):
            t = yy * CORES + 1 - core
            arrived(piece(ex, t), share_recv.at[ex * n_tp + t])

        @pl.loop(0, examples)
        def _(k):
            @pl.when(jnp.logical_and(d > 0, jnp.logical_or(zz != z, k >= BY_LINE)))
            def _():
                og_ready(chunk(zz, xx, k))

            add_example(ex, k)

    half = examples // 2
    relays(start)
    direct_parts(True)
    own_copies(start, 0, half)
    own_load().start()
    out_ref[...] = jnp.zeros_like(out_ref)
    relayed_parts(True)
    own_copies(start, half, examples)
    own_load().wait()

    @pl.loop(0, examples + slots)
    def _(i):
        s, k = 1 + i // examples, lax.rem(i, examples)

        @pl.when(s < line)
        def _():
            line_step(start, og_ready, s, k)

        @pl.when(i == 0)
        def _():
            side_copies(start, og_ready)

        n = i - examples
        at_slot(n + 2, act_parts)
        at_slot(n + 1, act_shares)
        at_slot(n, add_source)

    relays(sent)
    direct_parts(False)
    relayed_parts(False)
    own_copies(sent, 0, examples)

    @pl.loop(0, (line - 1) * examples)
    def _(i):
        line_step(sent, nothing, 1 + i // examples, lax.rem(i, examples))

    side_copies(sent, nothing)

    @pl.loop(0, n_ex)
    def _(ex):
        for d in range(1, ys):
            share_y(ex, d).wait_send()
        for yy in range(ys):
            share_core(ex, yy).wait_send()


def solution(mesh):
    n_ex, n_tp = mesh.shape["ex"], mesh.shape["tp"]

    def body(activations, out_grads):
        examples, tokens, width = out_grads.shape
        rows = width * n_tp // n_ex
        flat = activations.reshape(examples * tokens, width)
        chunks = n_ex * examples
        wide = n_ex // LINE
        ys = n_tp // CORES
        dma = pltpu.SemaphoreType.DMA
        return pl.pallas_call(
            functools.partial(kernel, n_ex, n_tp),
            out_shape=jax.ShapeDtypeStruct((rows, width), jnp.float32),
            in_specs=[pl.BlockSpec(memory_space=pltpu.HBM)] * 2,
            out_specs=pl.BlockSpec(memory_space=pltpu.VMEM),
            scratch_shapes=[
                pltpu.VMEM((n_ex, examples * tokens, rows), jnp.bfloat16),
                pltpu.VMEM((chunks, tokens, width), jnp.bfloat16),
                pltpu.VMEM((ys, CORES, examples * tokens // n_tp, width), jnp.bfloat16),
                pltpu.VMEM((rows, tokens), jnp.bfloat16),
                dma,
                dma((chunks,)),
                dma((chunks,)),
                dma((chunks,)),
                dma((chunks * wide,)),
                dma((width // rows * n_tp,)),
                dma((n_ex,)),
                dma((n_tp,)),
                dma((n_tp,)),
                dma((n_ex * ys,)),
                dma((n_ex * ys,)),
                dma((n_ex * n_tp,)),
            ],
            compiler_params=pltpu.CompilerParams(
                collective_id=0, has_side_effects=True, vmem_limit_bytes=40 * 1024 * 1024),
            cost_estimate=pl.CostEstimate(
                flops=2 * rows * width * chunks * tokens,
                bytes_accessed=12 * 1024 * 1024, transcendentals=0),
        )(flat, out_grads)

    return jax.shard_map(
        body,
        mesh=mesh,
        in_specs=(P("ex", None, "tp"), P("ex", None, "tp")),
        out_specs=P("ex", "tp"),
        check_vma=False,
    )
```

```python
import functools

import jax
import jax.numpy as jnp
from jax import lax
from jax.experimental import pallas as pl
from jax.experimental.pallas import tpu as pltpu
from jax.sharding import PartitionSpec as P

MESH = pl.DeviceIdType.MESH
LINE = 4
BY_LINE = 1
CORES = 2


def tile_of(size, most):
    while size % most:
        most //= 2
    return most


def kernel(n_ex, n_tp, act_ref, og_ref, out_ref, acts, ogs, relay, lhs,
           own_sem, og_recv, up_send, down_send, across_send,
           part_send, part_recv, relay_send, relay_recv, y_send, sib_send, share_recv):
    examples, tokens, width = og_ref.shape
    rows = out_ref.shape[0]
    line, wide = LINE, n_ex // LINE
    per_owner = width // rows
    ys = n_tp // CORES
    quarter = act_ref.shape[0] // n_tp

    me, tp = lax.axis_index("ex"), lax.axis_index("tp")
    z, x = me // wide, lax.rem(me, wide)
    y, core = tp // CORES, lax.rem(tp, CORES)
    owner = me // per_owner
    mine = lax.rem(owner, CORES) == core

    def chunk(zz, xx, k):
        return (zz * wide + xx) * examples + k

    def other(first, step, size):
        return lax.rem(first + step, size)

    barrier = pltpu.get_barrier_semaphore()

    def greet(ex, t):
        pl.semaphore_signal(barrier, inc=1, device_id={"ex": ex, "tp": t}, device_id_type=MESH)

    @pl.when(z > 0)
    def _():
        greet(me - wide, tp)

    @pl.when(z < line - 1)
    def _():
        greet(me + wide, tp)

    for d in range(1, wide):
        greet(z * wide + other(x, d, wide), tp)
    for d in range(1, ys):
        greet(me, other(y, d, ys) * CORES + core)
    greet(me, y * CORES + 1 - core)

    @pl.loop(0, n_ex)
    def _(ex):
        @pl.when(jnp.logical_not(jnp.logical_and(ex == me, mine)))
        def _():
            greet(ex, y * CORES + lax.rem(owner, CORES))

    count = (z > 0).astype(jnp.int32) + (z < line - 1).astype(jnp.int32) - mine.astype(jnp.int32)
    pl.semaphore_wait(barrier, count + (wide - 1) + (ys - 1) + 1 + per_owner * n_tp)

    def to_relay(d, c):
        to = other(y, d, ys)
        return pltpu.make_async_remote_copy(
            src_ref=act_ref.at[pl.ds((to * CORES + c) * quarter, quarter)], dst_ref=relay.at[y, c],
            send_sem=relay_send.at[d * CORES + c], recv_sem=relay_recv.at[y * CORES + c],
            device_id={"ex": me, "tp": to * CORES + core}, device_id_type=MESH)

    def part(source, from_y, c, j):
        t = y * CORES + c
        return pltpu.make_async_remote_copy(
            src_ref=source.at[:, pl.ds(j * rows, rows)],
            dst_ref=acts.at[me, pl.ds(t * quarter, quarter)],
            send_sem=part_send.at[(from_y * CORES + c) * per_owner + j], recv_sem=part_recv.at[me],
            device_id={"ex": (from_y * CORES + core) * per_owner + j, "tp": t}, device_id_type=MESH)

    def own_part(source, j):
        return pltpu.make_async_copy(
            source.at[:, pl.ds(j * rows, rows)],
            acts.at[me, pl.ds(tp * quarter, quarter)], part_recv.at[me])

    def parts_from(source, from_y, c, begin):
        for j in range(per_owner):
            itself = jnp.logical_and((from_y * CORES + core) * per_owner + j == me, c == core)

            @pl.when(jnp.logical_not(itself))
            def _():
                if begin:
                    part(source, from_y, c, j).start()
                else:
                    part(source, from_y, c, j).wait_send()

            if begin:
                @pl.when(itself)
                def _():
                    own_part(source, j).start()

    def direct_parts(begin):
        for c in range(CORES):
            parts_from(act_ref.at[pl.ds((y * CORES + c) * quarter, quarter)], y, c, begin)

    def relayed_parts(begin):
        for d in range(1, ys):
            from_y = other(y, d, ys)
            for c in range(CORES):
                if begin:
                    arrived(relay.at[from_y, c], relay_recv.at[from_y * CORES + c])
                parts_from(relay.at[from_y, c], from_y, c, begin)

    def relays(go):
        for d in range(1, ys):
            for c in range(CORES):
                go(to_relay(d, c))

    def piece(ex, t):
        return acts.at[ex, pl.ds(t * quarter, quarter)]

    def share_y(ex, d):
        return pltpu.make_async_remote_copy(
            src_ref=piece(ex, tp), dst_ref=piece(ex, tp),
            send_sem=y_send.at[ex * ys + d], recv_sem=share_recv.at[ex * n_tp + tp],
            device_id={"ex": me, "tp": other(y, d, ys) * CORES + core}, device_id_type=MESH)

    def share_core(ex, yy):
        t = yy * CORES + core
        return pltpu.make_async_remote_copy(
            src_ref=piece(ex, t), dst_ref=piece(ex, t),
            send_sem=sib_send.at[ex * ys + yy], recv_sem=share_recv.at[ex * n_tp + t],
            device_id={"ex": me, "tp": y * CORES + 1 - core}, device_id_type=MESH)

    def arrived(ref, sem):
        pltpu.make_async_copy(ref, ref, sem).wait()

    def og_copy(c, source, sems, slot, ex):
        return pltpu.make_async_remote_copy(
            src_ref=source, dst_ref=ogs.at[c], send_sem=sems.at[slot], recv_sem=og_recv.at[c],
            device_id={"ex": ex, "tp": tp}, device_id_type=MESH)

    def up(c, source):
        return og_copy(c, source, up_send, c, me + wide)

    def down(c, source):
        return og_copy(c, source, down_send, c, me - wide)

    def across(c, source, d):
        return og_copy(c, source, across_send, c * wide + d, z * wide + other(x, d, wide))

    def own_load():
        return pltpu.make_async_copy(og_ref, ogs.at[pl.ds(me * examples, examples)], own_sem)

    def own_copies(go, first, last):
        @pl.loop(first, last)
        def _(k):
            c = chunk(z, x, k)
            for d in range(1, wide):
                go(across(c, og_ref.at[k], d))

            @pl.when(z < line - 1)
            def _():
                go(up(c, og_ref.at[k]))

            @pl.when(z > 0)
            def _():
                go(down(c, og_ref.at[k]))

    def line_step(go, ready, s, k):
        for step in (-1, 1):
            zz = z + step * s

            @pl.when(jnp.logical_and(zz >= 0, zz < line))
            def _():
                c = chunk(zz, x, k)
                ready(c)
                if step < 0:
                    @pl.when(z < line - 1)
                    def _():
                        go(up(c, ogs.at[c]))
                else:
                    @pl.when(z > 0)
                    def _():
                        go(down(c, ogs.at[c]))

                @pl.when(jnp.logical_or(s > 1, k >= BY_LINE))
                def _():
                    for d in range(1, wide):
                        go(across(c, ogs.at[c], d))

    def side_ready():
        for k in range(BY_LINE):
            for d in range(1, wide):
                og_ready(chunk(z, other(x, d, wide), k))

    def side_copies(go):
        for k in range(BY_LINE):
            for d in range(1, wide):
                c = chunk(z, other(x, d, wide), k)

                @pl.when(z < line - 1)
                def _():
                    go(up(c, ogs.at[c]))

                @pl.when(z > 0)
                def _():
                    go(down(c, ogs.at[c]))

    def start(copy):
        copy.start()

    def sent(copy):
        copy.wait_send()

    def og_ready(c):
        arrived(ogs.at[c], og_recv.at[c])

    def nothing(c):
        pass

    def at_slot(n, act):
        far = n // wide
        below = jnp.minimum(z, line - 1 - z)
        near = jnp.where(lax.rem(far, 2) == 1, z - (far + 1) // 2, z + far // 2)
        end = jnp.where(z < line - 1 - z, far, line - 1 - far)
        zz = jnp.where(far <= 2 * below, near, end)
        d = lax.rem(n, wide)

        @pl.when(jnp.logical_and(n >= 0, n < n_ex))
        def _():
            act(d, zz, lax.rem(x + d, wide))

    def act_parts(d, zz, xx):
        ex = zz * wide + xx
        arrived(piece(ex, tp), part_recv.at[ex])
        for e in range(1, ys):
            share_y(ex, e).start()
        share_core(ex, y).start()

    def act_shares(d, zz, xx):
        ex = zz * wide + xx
        for e in range(1, ys):
            yy = other(y, e, ys)
            t = yy * CORES + core
            arrived(piece(ex, t), share_recv.at[ex * n_tp + t])
            share_core(ex, yy).start()

    col_tile = tile_of(width, 512)

    def add_example(ex, k):
        lhs[...] = acts[ex, pl.ds(pl.multiple_of(k * tokens, tokens), tokens), :].T

        @pl.loop(0, width // col_tile)
        def _(j):
            q = pl.ds(pl.multiple_of(j * col_tile, col_tile), col_tile)
            g = jnp.dot(lhs[...], ogs[ex * examples + k, :, q], preferred_element_type=jnp.float32)
            out_ref[:, q] += g * g

    def add_source(d, zz, xx):
        ex = zz * wide + xx
        for yy in range(ys):
            t = yy * CORES + 1 - core
            arrived(piece(ex, t), share_recv.at[ex * n_tp + t])

        @pl.loop(0, examples)
        def _(k):
            by_line = jnp.logical_and(jnp.logical_or(zz == z - 1, zz == z + 1), k < BY_LINE)
            across_here = jnp.logical_or(zz != z, k >= BY_LINE)

            @pl.when(jnp.logical_and(jnp.logical_and(d > 0, across_here), jnp.logical_not(by_line)))
            def _():
                og_ready(chunk(zz, xx, k))

            @pl.when(jnp.logical_not(jnp.logical_and(d > 0, by_line)))
            def _():
                add_example(ex, k)

    def add_by_line():
        for step in (-1, 1):
            zz = z + step

            @pl.when(jnp.logical_and(zz >= 0, zz < line))
            def _():
                @pl.loop(0, (wide - 1) * BY_LINE)
                def _(i):
                    xx, k = lax.rem(x + 1 + i // BY_LINE, wide), lax.rem(i, BY_LINE)
                    og_ready(chunk(zz, xx, k))
                    add_example(zz * wide + xx, k)

    half = examples // 2
    relays(start)
    direct_parts(True)
    own_copies(start, 0, half)
    own_load().start()
    out_ref[...] = jnp.zeros_like(out_ref)
    relayed_parts(True)
    own_copies(start, half, examples)
    own_load().wait()

    last = n_ex - wide

    @pl.loop(0, examples + n_ex + 1)
    def _(i):
        s, k = 1 + i // examples, lax.rem(i, examples)

        @pl.when(s < line)
        def _():
            line_step(start, og_ready, s, k)

        @pl.when(i == examples - 1)
        def _():
            side_ready()

        @pl.when(i == (line - 2) * examples)
        def _():
            side_copies(start)

        n = i - examples
        at_slot(n + 2, act_parts)
        at_slot(n + 1, act_shares)

        at_slot(jnp.where(n < last, n, jnp.where(n == last, -1, n - 1)), add_source)

    add_by_line()

    relays(sent)
    direct_parts(False)
    relayed_parts(False)
    own_copies(sent, 0, examples)

    @pl.loop(0, (line - 1) * examples)
    def _(i):
        line_step(sent, nothing, 1 + i // examples, lax.rem(i, examples))

    side_copies(sent)

    @pl.loop(0, n_ex)
    def _(ex):
        for d in range(1, ys):
            share_y(ex, d).wait_send()
        for yy in range(ys):
            share_core(ex, yy).wait_send()


def solution(mesh):
    n_ex, n_tp = mesh.shape["ex"], mesh.shape["tp"]

    def body(activations, out_grads):
        examples, tokens, width = out_grads.shape
        rows = width * n_tp // n_ex
        flat = activations.reshape(examples * tokens, width)
        chunks = n_ex * examples
        wide = n_ex // LINE
        ys = n_tp // CORES
        dma = pltpu.SemaphoreType.DMA
        return pl.pallas_call(
            functools.partial(kernel, n_ex, n_tp),
            out_shape=jax.ShapeDtypeStruct((rows, width), jnp.float32),
            in_specs=[pl.BlockSpec(memory_space=pltpu.HBM)] * 2,
            out_specs=pl.BlockSpec(memory_space=pltpu.VMEM),
            scratch_shapes=[
                pltpu.VMEM((n_ex, examples * tokens, rows), jnp.bfloat16),
                pltpu.VMEM((chunks, tokens, width), jnp.bfloat16),
                pltpu.VMEM((ys, CORES, examples * tokens // n_tp, width), jnp.bfloat16),
                pltpu.VMEM((rows, tokens), jnp.bfloat16),
                dma,
                dma((chunks,)),
                dma((chunks,)),
                dma((chunks,)),
                dma((chunks * wide,)),
                dma((width // rows * n_tp,)),
                dma((n_ex,)),
                dma((n_tp,)),
                dma((n_tp,)),
                dma((n_ex * ys,)),
                dma((n_ex * ys,)),
                dma((n_ex * n_tp,)),
            ],
            compiler_params=pltpu.CompilerParams(
                collective_id=0, has_side_effects=True, vmem_limit_bytes=40 * 1024 * 1024),
            cost_estimate=pl.CostEstimate(
                flops=2 * rows * width * chunks * tokens,
                bytes_accessed=12 * 1024 * 1024, transcendentals=0),
        )(flat, out_grads)

    return jax.shard_map(
        body,
        mesh=mesh,
        in_specs=(P("ex", None, "tp"), P("ex", None, "tp")),
        out_specs=P("ex", "tp"),
        check_vma=False,
    )
```

```python
import functools

import jax
import jax.numpy as jnp
from jax import lax
from jax.experimental import pallas as pl
from jax.experimental.pallas import tpu as pltpu
from jax.sharding import PartitionSpec as P

MESH = pl.DeviceIdType.MESH
LINE = 4
SPLIT = 2
BY_LINE = 3
CORES = 2


def tile_of(size, most):
    while size % most:
        most //= 2
    return most


def kernel(n_ex, n_tp, act_ref, og_ref, out_ref, acts, ogs, relay, lhs,
           own_sem, og_recv, up_send, down_send, across_send,
           part_send, part_recv, relay_send, relay_recv, y_send, sib_send, share_recv):
    examples, tokens, width = og_ref.shape
    rows = out_ref.shape[0]
    pieces, cut = examples * SPLIT, width // SPLIT
    line, wide = LINE, n_ex // LINE
    per_owner = width // rows
    ys = n_tp // CORES
    quarter = act_ref.shape[0] // n_tp

    me, tp = lax.axis_index("ex"), lax.axis_index("tp")
    z, x = me // wide, lax.rem(me, wide)
    y, core = tp // CORES, lax.rem(tp, CORES)
    owner = me // per_owner
    mine = lax.rem(owner, CORES) == core

    def chunk(zz, xx, k):
        return (zz * wide + xx) * pieces + k

    def other(first, step, size):
        return lax.rem(first + step, size)

    barrier = pltpu.get_barrier_semaphore()

    def greet(ex, t):
        pl.semaphore_signal(barrier, inc=1, device_id={"ex": ex, "tp": t}, device_id_type=MESH)

    @pl.when(z > 0)
    def _():
        greet(me - wide, tp)

    @pl.when(z < line - 1)
    def _():
        greet(me + wide, tp)

    for d in range(1, wide):
        greet(z * wide + other(x, d, wide), tp)
    for d in range(1, ys):
        greet(me, other(y, d, ys) * CORES + core)
    greet(me, y * CORES + 1 - core)

    @pl.loop(0, n_ex)
    def _(ex):
        @pl.when(jnp.logical_not(jnp.logical_and(ex == me, mine)))
        def _():
            greet(ex, y * CORES + lax.rem(owner, CORES))

    count = (z > 0).astype(jnp.int32) + (z < line - 1).astype(jnp.int32) - mine.astype(jnp.int32)
    pl.semaphore_wait(barrier, count + (wide - 1) + (ys - 1) + 1 + per_owner * n_tp)

    def to_relay(d, c):
        to = other(y, d, ys)
        return pltpu.make_async_remote_copy(
            src_ref=act_ref.at[pl.ds((to * CORES + c) * quarter, quarter)], dst_ref=relay.at[y, c],
            send_sem=relay_send.at[d * CORES + c], recv_sem=relay_recv.at[y * CORES + c],
            device_id={"ex": me, "tp": to * CORES + core}, device_id_type=MESH)

    def part(source, from_y, c, j):
        t = y * CORES + c
        return pltpu.make_async_remote_copy(
            src_ref=source.at[:, pl.ds(j * rows, rows)],
            dst_ref=acts.at[me, pl.ds(t * quarter, quarter)],
            send_sem=part_send.at[(from_y * CORES + c) * per_owner + j], recv_sem=part_recv.at[me],
            device_id={"ex": (from_y * CORES + core) * per_owner + j, "tp": t}, device_id_type=MESH)

    def own_part(source, j):
        return pltpu.make_async_copy(
            source.at[:, pl.ds(j * rows, rows)],
            acts.at[me, pl.ds(tp * quarter, quarter)], part_recv.at[me])

    def parts_from(source, from_y, c, begin):
        for j in range(per_owner):
            itself = jnp.logical_and((from_y * CORES + core) * per_owner + j == me, c == core)

            @pl.when(jnp.logical_not(itself))
            def _():
                if begin:
                    part(source, from_y, c, j).start()
                else:
                    part(source, from_y, c, j).wait_send()

            if begin:
                @pl.when(itself)
                def _():
                    own_part(source, j).start()

    def direct_parts(begin):
        for c in range(CORES):
            parts_from(act_ref.at[pl.ds((y * CORES + c) * quarter, quarter)], y, c, begin)

    def relayed_parts(begin):
        for d in range(1, ys):
            from_y = other(y, d, ys)
            for c in range(CORES):
                if begin:
                    arrived(relay.at[from_y, c], relay_recv.at[from_y * CORES + c])
                parts_from(relay.at[from_y, c], from_y, c, begin)

    def relays(go):
        for d in range(1, ys):
            for c in range(CORES):
                go(to_relay(d, c))

    def piece(ex, t):
        return acts.at[ex, pl.ds(t * quarter, quarter)]

    def share_y(ex, d):
        return pltpu.make_async_remote_copy(
            src_ref=piece(ex, tp), dst_ref=piece(ex, tp),
            send_sem=y_send.at[ex * ys + d], recv_sem=share_recv.at[ex * n_tp + tp],
            device_id={"ex": me, "tp": other(y, d, ys) * CORES + core}, device_id_type=MESH)

    def share_core(ex, yy):
        t = yy * CORES + core
        return pltpu.make_async_remote_copy(
            src_ref=piece(ex, t), dst_ref=piece(ex, t),
            send_sem=sib_send.at[ex * ys + yy], recv_sem=share_recv.at[ex * n_tp + t],
            device_id={"ex": me, "tp": y * CORES + 1 - core}, device_id_type=MESH)

    def arrived(ref, sem):
        pltpu.make_async_copy(ref, ref, sem).wait()

    def og_copy(c, source, sems, slot, ex):
        return pltpu.make_async_remote_copy(
            src_ref=source, dst_ref=ogs.at[c], send_sem=sems.at[slot], recv_sem=og_recv.at[c],
            device_id={"ex": ex, "tp": tp}, device_id_type=MESH)

    def up(c, source):
        return og_copy(c, source, up_send, c, me + wide)

    def down(c, source):
        return og_copy(c, source, down_send, c, me - wide)

    def across(c, source, d):
        return og_copy(c, source, across_send, c * wide + d, z * wide + other(x, d, wide))

    def own_load(h):
        return pltpu.make_async_copy(
            og_ref.at[:, :, pl.ds(h * cut, cut)],
            ogs.at[pl.ds(me * pieces + h * examples, examples)], own_sem.at[h])

    def own_copies(go, first, last):
        @pl.loop(first, last)
        def _(k):
            c = chunk(z, x, k)
            own = og_ref.at[lax.rem(k, examples), :, pl.ds(pl.multiple_of(k // examples * cut, cut), cut)]
            for d in range(1, wide):
                go(across(c, own, d))

            @pl.when(z < line - 1)
            def _():
                go(up(c, own))

            @pl.when(z > 0)
            def _():
                go(down(c, own))

    def line_step(go, ready, s, k):
        for step in (-1, 1):
            zz = z + step * s

            @pl.when(jnp.logical_and(zz >= 0, zz < line))
            def _():
                c = chunk(zz, x, k)
                ready(c)
                if step < 0:
                    @pl.when(z < line - 1)
                    def _():
                        go(up(c, ogs.at[c]))
                else:
                    @pl.when(z > 0)
                    def _():
                        go(down(c, ogs.at[c]))

                @pl.when(jnp.logical_or(s > 1, k >= BY_LINE))
                def _():
                    for d in range(1, wide):
                        go(across(c, ogs.at[c], d))

    def side_ready():
        for k in range(BY_LINE):
            for d in range(1, wide):
                og_ready(chunk(z, other(x, d, wide), k))

    def side_copies(go):
        for k in range(BY_LINE):
            for d in range(1, wide):
                c = chunk(z, other(x, d, wide), k)

                @pl.when(z < line - 1)
                def _():
                    go(up(c, ogs.at[c]))

                @pl.when(z > 0)
                def _():
                    go(down(c, ogs.at[c]))

    def start(copy):
        copy.start()

    def sent(copy):
        copy.wait_send()

    def og_ready(c):
        arrived(ogs.at[c], og_recv.at[c])

    def nothing(c):
        pass

    def at_slot(n, act):
        far = n // wide
        below = jnp.minimum(z, line - 1 - z)
        near = jnp.where(lax.rem(far, 2) == 1, z - (far + 1) // 2, z + far // 2)
        end = jnp.where(z < line - 1 - z, far, line - 1 - far)
        zz = jnp.where(far <= 2 * below, near, end)
        d = lax.rem(n, wide)

        @pl.when(jnp.logical_and(n >= 0, n < n_ex))
        def _():
            act(d, zz, lax.rem(x + d, wide))

    def act_parts(d, zz, xx):
        ex = zz * wide + xx
        arrived(piece(ex, tp), part_recv.at[ex])
        for e in range(1, ys):
            share_y(ex, e).start()
        share_core(ex, y).start()

    def act_shares(d, zz, xx):
        ex = zz * wide + xx
        for e in range(1, ys):
            yy = other(y, e, ys)
            t = yy * CORES + core
            arrived(piece(ex, t), share_recv.at[ex * n_tp + t])
            share_core(ex, yy).start()

    col_tile = tile_of(cut, 512)

    def add_piece(ex, u):
        k, h = lax.rem(u, examples), u // examples
        lhs[...] = acts[ex, pl.ds(pl.multiple_of(k * tokens, tokens), tokens), :].T

        @pl.loop(0, cut // col_tile)
        def _(j):
            q = pl.ds(pl.multiple_of(j * col_tile, col_tile), col_tile)
            to = pl.ds(pl.multiple_of(h * cut + j * col_tile, col_tile), col_tile)
            g = jnp.dot(lhs[...], ogs[ex * pieces + u, :, q], preferred_element_type=jnp.float32)
            out_ref[:, to] += g * g

    def add_source(d, zz, xx):
        ex = zz * wide + xx
        for yy in range(ys):
            t = yy * CORES + 1 - core
            arrived(piece(ex, t), share_recv.at[ex * n_tp + t])

        @pl.loop(0, pieces)
        def _(k):
            by_line = jnp.logical_and(jnp.logical_or(zz == z - 1, zz == z + 1), k < BY_LINE)
            across_here = jnp.logical_or(zz != z, k >= BY_LINE)

            @pl.when(jnp.logical_and(jnp.logical_and(d > 0, across_here), jnp.logical_not(by_line)))
            def _():
                og_ready(chunk(zz, xx, k))

            @pl.when(jnp.logical_not(jnp.logical_and(d > 0, by_line)))
            def _():
                add_piece(ex, k)

    def add_by_line():
        for step in (-1, 1):
            zz = z + step

            @pl.when(jnp.logical_and(zz >= 0, zz < line))
            def _():
                @pl.loop(0, (wide - 1) * BY_LINE)
                def _(i):
                    xx, k = lax.rem(x + 1 + i // BY_LINE, wide), lax.rem(i, BY_LINE)
                    og_ready(chunk(zz, xx, k))
                    add_piece(zz * wide + xx, k)

    half = pieces // 2
    relays(start)
    direct_parts(True)
    own_copies(start, 0, half)
    for h in range(SPLIT):
        own_load(h).start()
    out_ref[...] = jnp.zeros_like(out_ref)
    relayed_parts(True)
    own_copies(start, half, pieces)
    for h in range(SPLIT):
        own_load(h).wait()

    last = n_ex - wide

    @pl.loop(0, SPLIT * (examples + n_ex + 1))
    def _(i):
        s, k = 1 + i // pieces, lax.rem(i, pieces)

        @pl.when(s < line)
        def _():
            line_step(start, og_ready, s, k)

        @pl.when(i == pieces - 1)
        def _():
            side_ready()

        @pl.when(i == (line - 2) * pieces)
        def _():
            side_copies(start)

        @pl.when(lax.rem(i, SPLIT) == SPLIT - 1)
        def _():
            n = i // SPLIT - examples
            at_slot(n + 2, act_parts)
            at_slot(n + 1, act_shares)

            at_slot(jnp.where(n < last, n, jnp.where(n == last, -1, n - 1)), add_source)

    add_by_line()

    relays(sent)
    direct_parts(False)
    relayed_parts(False)
    own_copies(sent, 0, pieces)

    @pl.loop(0, (line - 1) * pieces)
    def _(i):
        line_step(sent, nothing, 1 + i // pieces, lax.rem(i, pieces))

    side_copies(sent)

    @pl.loop(0, n_ex)
    def _(ex):
        for d in range(1, ys):
            share_y(ex, d).wait_send()
        for yy in range(ys):
            share_core(ex, yy).wait_send()


def solution(mesh):
    n_ex, n_tp = mesh.shape["ex"], mesh.shape["tp"]

    def body(activations, out_grads):
        examples, tokens, width = out_grads.shape
        rows = width * n_tp // n_ex
        flat = activations.reshape(examples * tokens, width)
        chunks = n_ex * examples * SPLIT
        wide = n_ex // LINE
        ys = n_tp // CORES
        dma = pltpu.SemaphoreType.DMA
        return pl.pallas_call(
            functools.partial(kernel, n_ex, n_tp),
            out_shape=jax.ShapeDtypeStruct((rows, width), jnp.float32),
            in_specs=[pl.BlockSpec(memory_space=pltpu.HBM)] * 2,
            out_specs=pl.BlockSpec(memory_space=pltpu.VMEM),
            scratch_shapes=[
                pltpu.VMEM((n_ex, examples * tokens, rows), jnp.bfloat16),
                pltpu.VMEM((chunks, tokens, width // SPLIT), jnp.bfloat16),
                pltpu.VMEM((ys, CORES, examples * tokens // n_tp, width), jnp.bfloat16),
                pltpu.VMEM((rows, tokens), jnp.bfloat16),
                dma((SPLIT,)),
                dma((chunks,)),
                dma((chunks,)),
                dma((chunks,)),
                dma((chunks * wide,)),
                dma((width // rows * n_tp,)),
                dma((n_ex,)),
                dma((n_tp,)),
                dma((n_tp,)),
                dma((n_ex * ys,)),
                dma((n_ex * ys,)),
                dma((n_ex * n_tp,)),
            ],
            compiler_params=pltpu.CompilerParams(
                collective_id=0, has_side_effects=True, vmem_limit_bytes=40 * 1024 * 1024),
            cost_estimate=pl.CostEstimate(
                flops=2 * rows * width * n_ex * examples * tokens,
                bytes_accessed=12 * 1024 * 1024, transcendentals=0),
        )(
            pltpu.with_memory_space_constraint(flat, pltpu.HBM),
            pltpu.with_memory_space_constraint(out_grads, pltpu.HBM),
        )

    return jax.shard_map(
        body,
        mesh=mesh,
        in_specs=(P("ex", None, "tp"), P("ex", None, "tp")),
        out_specs=P("ex", "tp"),
        check_vma=False,
    )
```

```python
import functools

import jax
import jax.numpy as jnp
from jax import lax
from jax.experimental import pallas as pl
from jax.experimental.pallas import tpu as pltpu
from jax.sharding import PartitionSpec as P

MESH = pl.DeviceIdType.MESH
LINE = 4
SPLIT = 2
BY_LINE = 3
CORES = 2


def tile_of(size, most):
    while size % most:
        most //= 2
    return most


def kernel(n_ex, n_tp, act_ref, og_ref, out_ref, acts, ogs, relay, lhs,
           own_sem, og_recv, up_send, down_send, across_send,
           part_send, part_recv, relay_send, relay_recv, y_send, sib_send, share_recv):
    examples, tokens, width = og_ref.shape
    rows = out_ref.shape[0]
    pieces, cut = examples * SPLIT, width // SPLIT
    line, wide = LINE, n_ex // LINE
    per_owner = width // rows
    ys = n_tp // CORES
    quarter = act_ref.shape[0] // n_tp

    me, tp = lax.axis_index("ex"), lax.axis_index("tp")
    z, x = me // wide, lax.rem(me, wide)
    y, core = tp // CORES, lax.rem(tp, CORES)

    def chunk(zz, xx, k):
        return (zz * wide + xx) * pieces + k

    def other(first, step, size):
        return lax.rem(first + step, size)

    barrier = pltpu.get_barrier_semaphore()

    def greet(ex, t):
        pl.semaphore_signal(barrier, inc=1, device_id={"ex": ex, "tp": t}, device_id_type=MESH)

    for d in range(1, n_ex):
        greet(other(me, d, n_ex), tp)
    for d in range(1, n_tp):
        greet(me, other(tp, d, n_tp))
    pl.semaphore_wait(barrier, n_ex - 1 + n_tp - 1)

    def others():
        for dy in range(ys):
            for dc in range(CORES):
                if dy + dc:
                    yield dy * CORES + dc, other(y, dy, ys) * CORES + other(core, dc, CORES)

    def to_relay(slot, t):
        return pltpu.make_async_remote_copy(
            src_ref=act_ref.at[pl.ds(t * quarter, quarter)], dst_ref=relay.at[tp],
            send_sem=relay_send.at[slot], recv_sem=relay_recv.at[tp],
            device_id={"ex": me, "tp": t}, device_id_type=MESH)

    def part(source, ex, j):
        return pltpu.make_async_remote_copy(
            src_ref=source.at[:, pl.ds(j * rows, rows)], dst_ref=acts.at[me, pl.ds(tp * quarter, quarter)],
            send_sem=part_send.at[ex], recv_sem=part_recv.at[me],
            device_id={"ex": ex, "tp": tp}, device_id_type=MESH)

    def own_part(source, j):
        return pltpu.make_async_copy(
            source.at[:, pl.ds(j * rows, rows)],
            acts.at[me, pl.ds(tp * quarter, quarter)], part_recv.at[me])

    def parts_from(source, t, begin):
        for j in range(per_owner):
            ex = t * per_owner + j

            @pl.when(ex != me)
            def _():
                if begin:
                    part(source, ex, j).start()
                else:
                    part(source, ex, j).wait_send()

            if begin:
                @pl.when(ex == me)
                def _():
                    own_part(source, j).start()

    def direct_parts(begin):
        parts_from(act_ref.at[pl.ds(tp * quarter, quarter)], tp, begin)

    def relayed_parts(begin):
        for slot, t in others():
            if begin:
                arrived(relay.at[t], relay_recv.at[t])
            parts_from(relay.at[t], t, begin)

    def relays(go):
        for slot, t in others():
            go(to_relay(slot, t))

    def piece(ex, t):
        return acts.at[ex, pl.ds(t * quarter, quarter)]

    def share_y(ex, d):
        return pltpu.make_async_remote_copy(
            src_ref=piece(ex, tp), dst_ref=piece(ex, tp),
            send_sem=y_send.at[ex * ys + d], recv_sem=share_recv.at[ex * n_tp + tp],
            device_id={"ex": me, "tp": other(y, d, ys) * CORES + core}, device_id_type=MESH)

    def share_core(ex, yy):
        t = yy * CORES + core
        return pltpu.make_async_remote_copy(
            src_ref=piece(ex, t), dst_ref=piece(ex, t),
            send_sem=sib_send.at[ex * ys + yy], recv_sem=share_recv.at[ex * n_tp + t],
            device_id={"ex": me, "tp": y * CORES + 1 - core}, device_id_type=MESH)

    def arrived(ref, sem):
        pltpu.make_async_copy(ref, ref, sem).wait()

    def og_copy(c, source, sems, slot, ex):
        return pltpu.make_async_remote_copy(
            src_ref=source, dst_ref=ogs.at[c], send_sem=sems.at[slot], recv_sem=og_recv.at[c],
            device_id={"ex": ex, "tp": tp}, device_id_type=MESH)

    def up(c, source):
        return og_copy(c, source, up_send, c, me + wide)

    def down(c, source):
        return og_copy(c, source, down_send, c, me - wide)

    def across(c, source, d):
        return og_copy(c, source, across_send, c * wide + d, z * wide + other(x, d, wide))

    def own_load(h):
        return pltpu.make_async_copy(
            og_ref.at[:, :, pl.ds(h * cut, cut)],
            ogs.at[pl.ds(me * pieces + h * examples, examples)], own_sem.at[h])

    def own_copies(go, first, last):
        @pl.loop(first, last)
        def _(k):
            c = chunk(z, x, k)
            own = og_ref.at[lax.rem(k, examples), :, pl.ds(pl.multiple_of(k // examples * cut, cut), cut)]
            for d in range(1, wide):
                go(across(c, own, d))

            @pl.when(z < line - 1)
            def _():
                go(up(c, own))

            @pl.when(z > 0)
            def _():
                go(down(c, own))

    def line_step(go, ready, s, k):
        for step in (-1, 1):
            zz = z + step * s

            @pl.when(jnp.logical_and(zz >= 0, zz < line))
            def _():
                c = chunk(zz, x, k)
                ready(c)
                if step < 0:
                    @pl.when(z < line - 1)
                    def _():
                        go(up(c, ogs.at[c]))
                else:
                    @pl.when(z > 0)
                    def _():
                        go(down(c, ogs.at[c]))

                @pl.when(jnp.logical_or(s > 1, k >= BY_LINE))
                def _():
                    for d in range(1, wide):
                        go(across(c, ogs.at[c], d))

    def side_ready():
        for k in range(BY_LINE):
            for d in range(1, wide):
                og_ready(chunk(z, other(x, d, wide), k))

    def side_copies(go):
        for k in range(BY_LINE):
            for d in range(1, wide):
                c = chunk(z, other(x, d, wide), k)

                @pl.when(z < line - 1)
                def _():
                    go(up(c, ogs.at[c]))

                @pl.when(z > 0)
                def _():
                    go(down(c, ogs.at[c]))

    def start(copy):
        copy.start()

    def sent(copy):
        copy.wait_send()

    def og_ready(c):
        arrived(ogs.at[c], og_recv.at[c])

    def nothing(c):
        pass

    def at_slot(n, act):
        far = n // wide
        below = jnp.minimum(z, line - 1 - z)
        near = jnp.where(lax.rem(far, 2) == 1, z - (far + 1) // 2, z + far // 2)
        end = jnp.where(z < line - 1 - z, far, line - 1 - far)
        zz = jnp.where(far <= 2 * below, near, end)
        d = lax.rem(n, wide)

        @pl.when(jnp.logical_and(n >= 0, n < n_ex))
        def _():
            act(d, zz, lax.rem(x + d, wide))

    def act_parts(d, zz, xx):
        ex = zz * wide + xx
        arrived(piece(ex, tp), part_recv.at[ex])
        for e in range(1, ys):
            share_y(ex, e).start()
        share_core(ex, y).start()

    def act_shares(d, zz, xx):
        ex = zz * wide + xx
        for e in range(1, ys):
            yy = other(y, e, ys)
            t = yy * CORES + core
            arrived(piece(ex, t), share_recv.at[ex * n_tp + t])
            share_core(ex, yy).start()

    row_tile, col_tile = tile_of(rows, 256), tile_of(cut, 256)
    body = 2 * col_tile if cut % (2 * col_tile) == 0 else col_tile

    def turn(ex, k):
        lhs[k] = acts[ex, pl.ds(pl.multiple_of(k * tokens, tokens), tokens), :].T

    def add_piece(ex, u):
        k, h = lax.rem(u, examples), u // examples

        @pl.loop(0, cut // body)
        def _(i):
            for j in range(body // col_tile):
                start_at = i * body + j * col_tile
                q = pl.ds(pl.multiple_of(start_at, col_tile), col_tile)
                to = pl.ds(pl.multiple_of(h * cut + start_at, col_tile), col_tile)
                right = ogs[ex * pieces + u, :, q]
                for m in range(rows // row_tile):
                    r = pl.ds(m * row_tile, row_tile)
                    g = jnp.dot(lhs[k, r, :], right, preferred_element_type=jnp.float32)
                    out_ref[r, to] += g * g

    def add_source(d, zz, xx):
        ex = zz * wide + xx
        for yy in range(ys):
            t = yy * CORES + 1 - core
            arrived(piece(ex, t), share_recv.at[ex * n_tp + t])

        @pl.loop(0, examples)
        def _(k):
            turn(ex, k)

        @pl.loop(0, pieces)
        def _(k):
            by_line = jnp.logical_and(jnp.logical_or(zz == z - 1, zz == z + 1), k < BY_LINE)
            across_here = jnp.logical_or(zz != z, k >= BY_LINE)

            @pl.when(jnp.logical_and(jnp.logical_and(d > 0, across_here), jnp.logical_not(by_line)))
            def _():
                og_ready(chunk(zz, xx, k))

            @pl.when(jnp.logical_not(jnp.logical_and(d > 0, by_line)))
            def _():
                add_piece(ex, k)

    def add_by_line():
        for step in (-1, 1):
            zz = z + step

            @pl.when(jnp.logical_and(zz >= 0, zz < line))
            def _():
                @pl.loop(0, (wide - 1) * BY_LINE)
                def _(i):
                    xx, k = lax.rem(x + 1 + i // BY_LINE, wide), lax.rem(i, BY_LINE)
                    og_ready(chunk(zz, xx, k))
                    turn(zz * wide + xx, lax.rem(k, examples))
                    add_piece(zz * wide + xx, k)

    half = pieces // 2
    relays(start)
    direct_parts(True)
    own_copies(start, 0, half)
    for h in range(SPLIT):
        own_load(h).start()
    out_ref[...] = jnp.zeros_like(out_ref)
    relayed_parts(True)
    own_copies(start, half, pieces)
    for h in range(SPLIT):
        own_load(h).wait()

    last = n_ex - wide

    @pl.loop(0, SPLIT * (examples + n_ex + 1))
    def _(i):
        s, k = 1 + i // pieces, lax.rem(i, pieces)

        @pl.when(s < line)
        def _():
            line_step(start, og_ready, s, k)

        @pl.when(i == pieces - 1)
        def _():
            side_ready()

        @pl.when(i == (line - 2) * pieces)
        def _():
            side_copies(start)

        @pl.when(lax.rem(i, SPLIT) == SPLIT - 1)
        def _():
            n = i // SPLIT - examples
            at_slot(n + 2, act_parts)
            at_slot(n + 1, act_shares)

            at_slot(jnp.where(n < last, n, jnp.where(n == last, -1, n - 1)), add_source)

    add_by_line()

    relays(sent)
    direct_parts(False)
    relayed_parts(False)
    own_copies(sent, 0, pieces)

    @pl.loop(0, (line - 1) * pieces)
    def _(i):
        line_step(sent, nothing, 1 + i // pieces, lax.rem(i, pieces))

    side_copies(sent)

    @pl.loop(0, n_ex)
    def _(ex):
        for d in range(1, ys):
            share_y(ex, d).wait_send()
        for yy in range(ys):
            share_core(ex, yy).wait_send()


def solution(mesh):
    n_ex, n_tp = mesh.shape["ex"], mesh.shape["tp"]

    def body(activations, out_grads):
        examples, tokens, width = out_grads.shape
        rows = width * n_tp // n_ex
        flat = activations.reshape(examples * tokens, width)
        chunks = n_ex * examples * SPLIT
        wide = n_ex // LINE
        ys = n_tp // CORES
        dma = pltpu.SemaphoreType.DMA
        return pl.pallas_call(
            functools.partial(kernel, n_ex, n_tp),
            out_shape=jax.ShapeDtypeStruct((rows, width), jnp.float32),
            in_specs=[pl.BlockSpec(memory_space=pltpu.HBM)] * 2,
            out_specs=pl.BlockSpec(memory_space=pltpu.VMEM),
            scratch_shapes=[
                pltpu.VMEM((n_ex, examples * tokens, rows), jnp.bfloat16),
                pltpu.VMEM((chunks, tokens, width // SPLIT), jnp.bfloat16),
                pltpu.VMEM((n_tp, examples * tokens // n_tp, width), jnp.bfloat16),
                pltpu.VMEM((examples, rows, tokens), jnp.bfloat16),
                dma((SPLIT,)),
                dma((chunks,)),
                dma((chunks,)),
                dma((chunks,)),
                dma((chunks * wide,)),
                dma((n_ex,)),
                dma((n_ex,)),
                dma((n_tp,)),
                dma((n_tp,)),
                dma((n_ex * ys,)),
                dma((n_ex * ys,)),
                dma((n_ex * n_tp,)),
            ],
            compiler_params=pltpu.CompilerParams(
                collective_id=0, has_side_effects=True, vmem_limit_bytes=40 * 1024 * 1024),
            cost_estimate=pl.CostEstimate(
                flops=2 * rows * width * n_ex * examples * tokens,
                bytes_accessed=12 * 1024 * 1024, transcendentals=0),
        )(
            pltpu.with_memory_space_constraint(flat, pltpu.HBM),
            pltpu.with_memory_space_constraint(out_grads, pltpu.HBM),
        )

    return jax.shard_map(
        body,
        mesh=mesh,
        in_specs=(P("ex", None, "tp"), P("ex", None, "tp")),
        out_specs=P("ex", "tp"),
        check_vma=False,
    )
```

```python
import functools

import jax
import jax.numpy as jnp
from jax import lax
from jax.experimental import pallas as pl
from jax.experimental.pallas import tpu as pltpu
from jax.sharding import PartitionSpec as P

MESH = pl.DeviceIdType.MESH
LINE = 4
SPLIT = 2
BY_LINE = 2
CORES = 2


def tile_of(size, most):
    while size % most:
        most //= 2
    return most


def kernel(n_ex, n_tp, act_ref, og_ref, out_ref, acts, ogs, relay, lhs,
           own_sem, og_recv, up_send, down_send, across_send,
           part_send, part_recv, relay_send, relay_recv, y_send, sib_send, share_recv):
    examples, tokens, width = og_ref.shape
    rows = out_ref.shape[0]
    pieces, cut = examples * SPLIT, width // SPLIT
    line, wide = LINE, n_ex // LINE
    per_owner = width // rows
    ys = n_tp // CORES
    quarter = act_ref.shape[0] // n_tp

    me, tp = lax.axis_index("ex"), lax.axis_index("tp")
    z, x = me // wide, lax.rem(me, wide)
    y, core = tp // CORES, lax.rem(tp, CORES)

    def chunk(zz, xx, k):
        return (zz * wide + xx) * pieces + k

    def other(first, step, size):
        return lax.rem(first + step, size)

    barrier = pltpu.get_barrier_semaphore()

    def greet(ex, t):
        pl.semaphore_signal(barrier, inc=1, device_id={"ex": ex, "tp": t}, device_id_type=MESH)

    for d in range(1, n_ex):
        greet(other(me, d, n_ex), tp)
    for d in range(1, n_tp):
        greet(me, other(tp, d, n_tp))
    pl.semaphore_wait(barrier, n_ex - 1 + n_tp - 1)

    def others():
        for dy in range(ys):
            for dc in range(CORES):
                if dy + dc:
                    yield dy * CORES + dc, other(y, dy, ys) * CORES + other(core, dc, CORES)

    def to_relay(slot, t):
        return pltpu.make_async_remote_copy(
            src_ref=act_ref.at[pl.ds(t * quarter, quarter)], dst_ref=relay.at[tp],
            send_sem=relay_send.at[slot], recv_sem=relay_recv.at[tp],
            device_id={"ex": me, "tp": t}, device_id_type=MESH)

    def part(source, ex, j):
        return pltpu.make_async_remote_copy(
            src_ref=source.at[:, pl.ds(j * rows, rows)], dst_ref=acts.at[me, pl.ds(tp * quarter, quarter)],
            send_sem=part_send.at[ex], recv_sem=part_recv.at[me],
            device_id={"ex": ex, "tp": tp}, device_id_type=MESH)

    def own_part(source, j):
        return pltpu.make_async_copy(
            source.at[:, pl.ds(j * rows, rows)],
            acts.at[me, pl.ds(tp * quarter, quarter)], part_recv.at[me])

    def parts_from(source, t, begin):
        for j in range(per_owner):
            ex = t * per_owner + j

            @pl.when(ex != me)
            def _():
                if begin:
                    part(source, ex, j).start()
                else:
                    part(source, ex, j).wait_send()

            if begin:
                @pl.when(ex == me)
                def _():
                    own_part(source, j).start()

    def direct_parts(begin):
        parts_from(act_ref.at[pl.ds(tp * quarter, quarter)], tp, begin)

    def relayed_parts(begin):
        for slot, t in others():
            if begin:
                arrived(relay.at[t], relay_recv.at[t])
            parts_from(relay.at[t], t, begin)

    def relays(go):
        for slot, t in others():
            go(to_relay(slot, t))

    def piece(ex, t):
        return acts.at[ex, pl.ds(t * quarter, quarter)]

    def share_y(ex, d):
        return pltpu.make_async_remote_copy(
            src_ref=piece(ex, tp), dst_ref=piece(ex, tp),
            send_sem=y_send.at[ex * ys + d], recv_sem=share_recv.at[ex * n_tp + tp],
            device_id={"ex": me, "tp": other(y, d, ys) * CORES + core}, device_id_type=MESH)

    def share_core(ex, yy):
        t = yy * CORES + core
        return pltpu.make_async_remote_copy(
            src_ref=piece(ex, t), dst_ref=piece(ex, t),
            send_sem=sib_send.at[ex * ys + yy], recv_sem=share_recv.at[ex * n_tp + t],
            device_id={"ex": me, "tp": y * CORES + 1 - core}, device_id_type=MESH)

    def arrived(ref, sem):
        pltpu.make_async_copy(ref, ref, sem).wait()

    def og_copy(c, source, sems, slot, ex):
        return pltpu.make_async_remote_copy(
            src_ref=source, dst_ref=ogs.at[c], send_sem=sems.at[slot], recv_sem=og_recv.at[c],
            device_id={"ex": ex, "tp": tp}, device_id_type=MESH)

    def up(c, source):
        return og_copy(c, source, up_send, c, me + wide)

    def down(c, source):
        return og_copy(c, source, down_send, c, me - wide)

    def across(c, source, d):
        return og_copy(c, source, across_send, c * wide + d, z * wide + other(x, d, wide))

    def own_load(h):
        return pltpu.make_async_copy(
            og_ref.at[:, :, pl.ds(h * cut, cut)],
            ogs.at[pl.ds(me * pieces + h * examples, examples)], own_sem.at[h])

    def own_copies(go, first, last):
        @pl.loop(first, last)
        def _(k):
            c = chunk(z, x, k)
            own = og_ref.at[lax.rem(k, examples), :, pl.ds(pl.multiple_of(k // examples * cut, cut), cut)]
            for d in range(1, wide):
                go(across(c, own, d))

            @pl.when(z < line - 1)
            def _():
                go(up(c, own))

            @pl.when(z > 0)
            def _():
                go(down(c, own))

    def line_step(go, ready, s, k):
        for step in (-1, 1):
            zz = z + step * s

            @pl.when(jnp.logical_and(zz >= 0, zz < line))
            def _():
                c = chunk(zz, x, k)
                ready(c)
                if step < 0:
                    @pl.when(z < line - 1)
                    def _():
                        go(up(c, ogs.at[c]))
                else:
                    @pl.when(z > 0)
                    def _():
                        go(down(c, ogs.at[c]))

                @pl.when(jnp.logical_or(s > 1, k >= BY_LINE))
                def _():
                    for d in range(1, wide):
                        go(across(c, ogs.at[c], d))

    def side_ready():
        for k in range(BY_LINE):
            for d in range(1, wide):
                og_ready(chunk(z, other(x, d, wide), k))

    def side_copies(go):
        for k in range(BY_LINE):
            for d in range(1, wide):
                c = chunk(z, other(x, d, wide), k)

                @pl.when(z < line - 1)
                def _():
                    go(up(c, ogs.at[c]))

                @pl.when(z > 0)
                def _():
                    go(down(c, ogs.at[c]))

    def start(copy):
        copy.start()

    def sent(copy):
        copy.wait_send()

    def og_ready(c):
        arrived(ogs.at[c], og_recv.at[c])

    def nothing(c):
        pass

    def at_slot(n, act):
        far = n // wide
        below = jnp.minimum(z, line - 1 - z)
        near = jnp.where(lax.rem(far, 2) == 1, z - (far + 1) // 2, z + far // 2)
        end = jnp.where(z < line - 1 - z, far, line - 1 - far)
        zz = jnp.where(far <= 2 * below, near, end)
        d = lax.rem(n, wide)

        @pl.when(jnp.logical_and(n >= 0, n < n_ex))
        def _():
            act(d, zz, lax.rem(x + d, wide))

    def act_parts(d, zz, xx):
        ex = zz * wide + xx
        arrived(piece(ex, tp), part_recv.at[ex])
        for e in range(1, ys):
            share_y(ex, e).start()
        share_core(ex, y).start()

    def act_shares(d, zz, xx):
        ex = zz * wide + xx
        for e in range(1, ys):
            yy = other(y, e, ys)
            t = yy * CORES + core
            arrived(piece(ex, t), share_recv.at[ex * n_tp + t])
            share_core(ex, yy).start()

    row_tile, col_tile = tile_of(rows, 256), tile_of(cut, 256)
    body = 2 * col_tile if cut % (2 * col_tile) == 0 else col_tile

    def turn(ex, k):
        lhs[k] = acts[ex, pl.ds(pl.multiple_of(k * tokens, tokens), tokens), :].T

    def add_piece(ex, u):
        k, h = lax.rem(u, examples), u // examples

        @pl.loop(0, cut // body)
        def _(i):
            for j in range(body // col_tile):
                start_at = i * body + j * col_tile
                q = pl.ds(pl.multiple_of(start_at, col_tile), col_tile)
                to = pl.ds(pl.multiple_of(h * cut + start_at, col_tile), col_tile)
                right = ogs[ex * pieces + u, :, q]
                for m in range(rows // row_tile):
                    r = pl.ds(m * row_tile, row_tile)
                    g = jnp.dot(lhs[k, r, :], right, preferred_element_type=jnp.float32)
                    out_ref[r, to] += g * g

    def add_source(d, zz, xx):
        ex = zz * wide + xx
        for yy in range(ys):
            t = yy * CORES + 1 - core
            arrived(piece(ex, t), share_recv.at[ex * n_tp + t])

        @pl.loop(0, examples)
        def _(k):
            turn(ex, k)

        @pl.loop(0, pieces)
        def _(k):
            by_line = jnp.logical_and(jnp.logical_or(zz == z - 1, zz == z + 1), k < BY_LINE)
            across_here = jnp.logical_or(zz != z, k >= BY_LINE)

            @pl.when(jnp.logical_and(jnp.logical_and(d > 0, across_here), jnp.logical_not(by_line)))
            def _():
                og_ready(chunk(zz, xx, k))

            @pl.when(jnp.logical_not(jnp.logical_and(d > 0, by_line)))
            def _():
                add_piece(ex, k)

    def add_by_line():
        for step in (-1, 1):
            zz = z + step

            @pl.when(jnp.logical_and(zz >= 0, zz < line))
            def _():
                @pl.loop(0, (wide - 1) * BY_LINE)
                def _(i):
                    xx, k = lax.rem(x + 1 + i // BY_LINE, wide), lax.rem(i, BY_LINE)
                    og_ready(chunk(zz, xx, k))
                    turn(zz * wide + xx, lax.rem(k, examples))
                    add_piece(zz * wide + xx, k)

    half = pieces // 2
    relays(start)
    direct_parts(True)
    own_copies(start, 0, half)
    for h in range(SPLIT):
        own_load(h).start()
    out_ref[...] = jnp.zeros_like(out_ref)
    relayed_parts(True)
    own_copies(start, half, pieces)
    for h in range(SPLIT):
        own_load(h).wait()

    last = n_ex - wide

    @pl.loop(0, SPLIT * (examples + n_ex + 1))
    def _(i):
        s, k = 1 + i // pieces, lax.rem(i, pieces)

        @pl.when(s < line)
        def _():
            line_step(start, og_ready, s, k)

        @pl.when(i == pieces - 1)
        def _():
            side_ready()

        @pl.when(i == (line - 2) * pieces)
        def _():
            side_copies(start)

        @pl.when(lax.rem(i, SPLIT) == SPLIT - 1)
        def _():
            n = i // SPLIT - examples
            at_slot(n + 2, act_parts)
            at_slot(n + 1, act_shares)

            @pl.when(n == n_ex)
            def _():
                add_by_line()

            at_slot(jnp.where(n < last, n, jnp.where(n == last, -1, n - 1)), add_source)

    relays(sent)
    direct_parts(False)
    relayed_parts(False)
    own_copies(sent, 0, pieces)

    @pl.loop(0, (line - 1) * pieces)
    def _(i):
        line_step(sent, nothing, 1 + i // pieces, lax.rem(i, pieces))

    side_copies(sent)

    @pl.loop(0, n_ex)
    def _(ex):
        for d in range(1, ys):
            share_y(ex, d).wait_send()
        for yy in range(ys):
            share_core(ex, yy).wait_send()


def solution(mesh):
    n_ex, n_tp = mesh.shape["ex"], mesh.shape["tp"]

    def body(activations, out_grads):
        examples, tokens, width = out_grads.shape
        rows = width * n_tp // n_ex
        flat = activations.reshape(examples * tokens, width)
        chunks = n_ex * examples * SPLIT
        wide = n_ex // LINE
        ys = n_tp // CORES
        dma = pltpu.SemaphoreType.DMA
        return pl.pallas_call(
            functools.partial(kernel, n_ex, n_tp),
            out_shape=jax.ShapeDtypeStruct((rows, width), jnp.float32),
            in_specs=[pl.BlockSpec(memory_space=pltpu.HBM)] * 2,
            out_specs=pl.BlockSpec(memory_space=pltpu.VMEM),
            scratch_shapes=[
                pltpu.VMEM((n_ex, examples * tokens, rows), jnp.bfloat16),
                pltpu.VMEM((chunks, tokens, width // SPLIT), jnp.bfloat16),
                pltpu.VMEM((n_tp, examples * tokens // n_tp, width), jnp.bfloat16),
                pltpu.VMEM((examples, rows, tokens), jnp.bfloat16),
                dma((SPLIT,)),
                dma((chunks,)),
                dma((chunks,)),
                dma((chunks,)),
                dma((chunks * wide,)),
                dma((n_ex,)),
                dma((n_ex,)),
                dma((n_tp,)),
                dma((n_tp,)),
                dma((n_ex * ys,)),
                dma((n_ex * ys,)),
                dma((n_ex * n_tp,)),
            ],
            compiler_params=pltpu.CompilerParams(
                collective_id=0, has_side_effects=True, vmem_limit_bytes=40 * 1024 * 1024),
            cost_estimate=pl.CostEstimate(
                flops=2 * rows * width * n_ex * examples * tokens,
                bytes_accessed=12 * 1024 * 1024, transcendentals=0),
        )(
            pltpu.with_memory_space_constraint(flat, pltpu.HBM),
            pltpu.with_memory_space_constraint(out_grads, pltpu.HBM),
        )

    return jax.shard_map(
        body,
        mesh=mesh,
        in_specs=(P("ex", None, "tp"), P("ex", None, "tp")),
        out_specs=P("ex", "tp"),
        check_vma=False,
    )
```

```python
import functools

import jax
import jax.numpy as jnp
from jax import lax
from jax.experimental import pallas as pl
from jax.experimental.pallas import tpu as pltpu
from jax.sharding import PartitionSpec as P

MESH = pl.DeviceIdType.MESH
LINE = 4
SPLIT = 2
BY_LINE = 3
CORES = 2


def tile_of(size, most):
    while size % most:
        most //= 2
    return most


def kernel(n_ex, n_tp, act_ref, og_ref, out_ref, acts, ogs, relay, lhs,
           own_sem, og_recv, up_send, down_send, across_send,
           part_send, part_recv, relay_send, relay_recv, y_send, sib_send, share_recv):
    examples, tokens, width = og_ref.shape
    rows = out_ref.shape[0]
    pieces, cut = examples * SPLIT, width // SPLIT
    line, wide = LINE, n_ex // LINE
    per_owner = width // rows
    ys = n_tp // CORES
    quarter = act_ref.shape[0] // n_tp

    me, tp = lax.axis_index("ex"), lax.axis_index("tp")
    z, x = me // wide, lax.rem(me, wide)
    y, core = tp // CORES, lax.rem(tp, CORES)

    def chunk(zz, xx, k):
        return (zz * wide + xx) * pieces + k

    def other(first, step, size):
        return lax.rem(first + step, size)

    barrier = pltpu.get_barrier_semaphore()

    def greet(ex, t):
        pl.semaphore_signal(barrier, inc=1, device_id={"ex": ex, "tp": t}, device_id_type=MESH)

    for d in range(1, n_ex):
        greet(other(me, d, n_ex), tp)
    for d in range(1, n_tp):
        greet(me, other(tp, d, n_tp))
    pl.semaphore_wait(barrier, n_ex - 1 + n_tp - 1)

    def others():
        for dy in range(ys):
            for dc in range(CORES):
                if dy + dc:
                    yield dy * CORES + dc, other(y, dy, ys) * CORES + other(core, dc, CORES)

    def to_relay(slot, t):
        return pltpu.make_async_remote_copy(
            src_ref=act_ref.at[pl.ds(t * quarter, quarter)], dst_ref=relay.at[tp],
            send_sem=relay_send.at[slot], recv_sem=relay_recv.at[tp],
            device_id={"ex": me, "tp": t}, device_id_type=MESH)

    def part(source, ex, j):
        return pltpu.make_async_remote_copy(
            src_ref=source.at[:, pl.ds(j * rows, rows)], dst_ref=acts.at[me, pl.ds(tp * quarter, quarter)],
            send_sem=part_send.at[ex], recv_sem=part_recv.at[me],
            device_id={"ex": ex, "tp": tp}, device_id_type=MESH)

    def own_part(source, j):
        return pltpu.make_async_copy(
            source.at[:, pl.ds(j * rows, rows)],
            acts.at[me, pl.ds(tp * quarter, quarter)], part_recv.at[me])

    def parts_from(source, t, begin):
        for j in range(per_owner):
            ex = t * per_owner + j

            @pl.when(ex != me)
            def _():
                if begin:
                    part(source, ex, j).start()
                else:
                    part(source, ex, j).wait_send()

            if begin:
                @pl.when(ex == me)
                def _():
                    own_part(source, j).start()

    def direct_parts(begin):
        parts_from(act_ref.at[pl.ds(tp * quarter, quarter)], tp, begin)

    def relayed_parts(begin):
        for slot, t in others():
            if begin:
                arrived(relay.at[t], relay_recv.at[t])
            parts_from(relay.at[t], t, begin)

    def relays(go):
        for slot, t in others():
            go(to_relay(slot, t))

    def piece(ex, t):
        return acts.at[ex, pl.ds(t * quarter, quarter)]

    def share_y(ex, d):
        return pltpu.make_async_remote_copy(
            src_ref=piece(ex, tp), dst_ref=piece(ex, tp),
            send_sem=y_send.at[ex * ys + d], recv_sem=share_recv.at[ex * n_tp + tp],
            device_id={"ex": me, "tp": other(y, d, ys) * CORES + core}, device_id_type=MESH)

    def share_core(ex, yy):
        t = yy * CORES + core
        return pltpu.make_async_remote_copy(
            src_ref=piece(ex, t), dst_ref=piece(ex, t),
            send_sem=sib_send.at[ex * ys + yy], recv_sem=share_recv.at[ex * n_tp + t],
            device_id={"ex": me, "tp": y * CORES + 1 - core}, device_id_type=MESH)

    def arrived(ref, sem):
        pltpu.make_async_copy(ref, ref, sem).wait()

    def og_copy(c, source, sems, slot, ex):
        return pltpu.make_async_remote_copy(
            src_ref=source, dst_ref=ogs.at[c], send_sem=sems.at[slot], recv_sem=og_recv.at[c],
            device_id={"ex": ex, "tp": tp}, device_id_type=MESH)

    def up(c, source):
        return og_copy(c, source, up_send, c, me + wide)

    def down(c, source):
        return og_copy(c, source, down_send, c, me - wide)

    def across(c, source, d):
        return og_copy(c, source, across_send, c * wide + d, z * wide + other(x, d, wide))

    def own_load(h):
        return pltpu.make_async_copy(
            og_ref.at[:, :, pl.ds(h * cut, cut)],
            ogs.at[pl.ds(me * pieces + h * examples, examples)], own_sem.at[h])

    def own_copies(go, first, last):
        @pl.loop(first, last)
        def _(k):
            c = chunk(z, x, k)
            own = og_ref.at[lax.rem(k, examples), :, pl.ds(pl.multiple_of(k // examples * cut, cut), cut)]
            for d in range(1, wide):
                go(across(c, own, d))

            @pl.when(z < line - 1)
            def _():
                go(up(c, own))

            @pl.when(z > 0)
            def _():
                go(down(c, own))

    def line_step(go, ready, s, k):
        for step in (-1, 1):
            zz = z + step * s

            @pl.when(jnp.logical_and(zz >= 0, zz < line))
            def _():
                c = chunk(zz, x, k)
                ready(c)
                if step < 0:
                    @pl.when(z < line - 1)
                    def _():
                        go(up(c, ogs.at[c]))
                else:
                    @pl.when(z > 0)
                    def _():
                        go(down(c, ogs.at[c]))

                @pl.when(jnp.logical_or(s > 1, k >= BY_LINE))
                def _():
                    for d in range(1, wide):
                        go(across(c, ogs.at[c], d))

    def side_ready():
        for k in range(BY_LINE):
            for d in range(1, wide):
                og_ready(chunk(z, other(x, d, wide), k))

    def side_copies(go):
        for k in range(BY_LINE):
            for d in range(1, wide):
                c = chunk(z, other(x, d, wide), k)

                @pl.when(z < line - 1)
                def _():
                    go(up(c, ogs.at[c]))

                @pl.when(z > 0)
                def _():
                    go(down(c, ogs.at[c]))

    def start(copy):
        copy.start()

    def sent(copy):
        copy.wait_send()

    def og_ready(c):
        arrived(ogs.at[c], og_recv.at[c])

    def nothing(c):
        pass

    def at_slot(n, act):
        far = n // wide
        below = jnp.minimum(z, line - 1 - z)
        near = jnp.where(lax.rem(far, 2) == 1, z - (far + 1) // 2, z + far // 2)
        end = jnp.where(z < line - 1 - z, far, line - 1 - far)
        zz = jnp.where(far <= 2 * below, near, end)
        d = lax.rem(n, wide)

        @pl.when(jnp.logical_and(n >= 0, n < n_ex))
        def _():
            act(d, zz, lax.rem(x + d, wide))

    def act_parts(d, zz, xx):
        ex = zz * wide + xx
        arrived(piece(ex, tp), part_recv.at[ex])
        for e in range(1, ys):
            share_y(ex, e).start()
        share_core(ex, y).start()

    def act_shares(d, zz, xx):
        ex = zz * wide + xx
        for e in range(1, ys):
            yy = other(y, e, ys)
            t = yy * CORES + core
            arrived(piece(ex, t), share_recv.at[ex * n_tp + t])
            share_core(ex, yy).start()

    row_tile, col_tile = tile_of(rows, 256), tile_of(cut, 256)
    body = 2 * col_tile if cut % (2 * col_tile) == 0 else col_tile

    def turn(ex, k):
        lhs[k] = acts[ex, pl.ds(pl.multiple_of(k * tokens, tokens), tokens), :].T

    def add_piece(ex, u):
        k, h = lax.rem(u, examples), u // examples

        @pl.loop(0, cut // body)
        def _(i):
            for j in range(body // col_tile):
                start_at = i * body + j * col_tile
                q = pl.ds(pl.multiple_of(start_at, col_tile), col_tile)
                to = pl.ds(pl.multiple_of(h * cut + start_at, col_tile), col_tile)
                right = ogs[ex * pieces + u, :, q]
                for m in range(rows // row_tile):
                    r = pl.ds(m * row_tile, row_tile)
                    g = jnp.dot(lhs[k, r, :], right, preferred_element_type=jnp.float32)
                    out_ref[r, to] += g * g

    def add_source(d, zz, xx):
        ex = zz * wide + xx
        for yy in range(ys):
            t = yy * CORES + 1 - core
            arrived(piece(ex, t), share_recv.at[ex * n_tp + t])

        @pl.loop(0, examples)
        def _(k):
            turn(ex, k)

        @pl.loop(0, pieces)
        def _(k):
            by_line = jnp.logical_and(jnp.logical_or(zz == z - 1, zz == z + 1), k < BY_LINE)
            across_here = jnp.logical_or(zz != z, k >= BY_LINE)

            @pl.when(jnp.logical_and(jnp.logical_and(d > 0, across_here), jnp.logical_not(by_line)))
            def _():
                og_ready(chunk(zz, xx, k))

            @pl.when(jnp.logical_not(jnp.logical_and(d > 0, by_line)))
            def _():
                add_piece(ex, k)

    def add_by_line():
        for step in (-1, 1):
            zz = z + step

            @pl.when(jnp.logical_and(zz >= 0, zz < line))
            def _():
                @pl.loop(1, wide)
                def _(d):
                    xx = lax.rem(x + d, wide)

                    @pl.loop(0, min(BY_LINE, examples))
                    def _(k):
                        turn(zz * wide + xx, k)

                    @pl.loop(0, BY_LINE)
                    def _(k):
                        og_ready(chunk(zz, xx, k))
                        add_piece(zz * wide + xx, k)

    half = pieces // 2
    relays(start)
    direct_parts(True)
    own_copies(start, 0, half)
    for h in range(SPLIT):
        own_load(h).start()
    out_ref[...] = jnp.zeros_like(out_ref)
    relayed_parts(True)
    own_copies(start, half, pieces)
    for h in range(SPLIT):
        own_load(h).wait()

    last = n_ex - wide

    @pl.loop(0, SPLIT * (examples + n_ex + 1))
    def _(i):
        s, k = 1 + i // pieces, lax.rem(i, pieces)

        @pl.when(s < line)
        def _():
            line_step(start, og_ready, s, k)

        @pl.when(i == pieces - 1)
        def _():
            side_ready()

        @pl.when(i == (line - 2) * pieces)
        def _():
            side_copies(start)

        @pl.when(lax.rem(i, SPLIT) == SPLIT - 1)
        def _():
            n = i // SPLIT - examples
            at_slot(n + 2, act_parts)
            at_slot(n + 1, act_shares)

            at_slot(jnp.where(n < last, n, jnp.where(n == last, -1, n - 1)), add_source)

    add_by_line()

    relays(sent)
    direct_parts(False)
    relayed_parts(False)
    own_copies(sent, 0, pieces)

    @pl.loop(0, (line - 1) * pieces)
    def _(i):
        line_step(sent, nothing, 1 + i // pieces, lax.rem(i, pieces))

    side_copies(sent)

    @pl.loop(0, n_ex)
    def _(ex):
        for d in range(1, ys):
            share_y(ex, d).wait_send()
        for yy in range(ys):
            share_core(ex, yy).wait_send()


def solution(mesh):
    n_ex, n_tp = mesh.shape["ex"], mesh.shape["tp"]

    def body(activations, out_grads):
        examples, tokens, width = out_grads.shape
        rows = width * n_tp // n_ex
        flat = activations.reshape(examples * tokens, width)
        chunks = n_ex * examples * SPLIT
        wide = n_ex // LINE
        ys = n_tp // CORES
        dma = pltpu.SemaphoreType.DMA
        return pl.pallas_call(
            functools.partial(kernel, n_ex, n_tp),
            out_shape=jax.ShapeDtypeStruct((rows, width), jnp.float32),
            in_specs=[pl.BlockSpec(memory_space=pltpu.HBM)] * 2,
            out_specs=pl.BlockSpec(memory_space=pltpu.VMEM),
            scratch_shapes=[
                pltpu.VMEM((n_ex, examples * tokens, rows), jnp.bfloat16),
                pltpu.VMEM((chunks, tokens, width // SPLIT), jnp.bfloat16),
                pltpu.VMEM((n_tp, examples * tokens // n_tp, width), jnp.bfloat16),
                pltpu.VMEM((examples, rows, tokens), jnp.bfloat16),
                dma((SPLIT,)),
                dma((chunks,)),
                dma((chunks,)),
                dma((chunks,)),
                dma((chunks * wide,)),
                dma((n_ex,)),
                dma((n_ex,)),
                dma((n_tp,)),
                dma((n_tp,)),
                dma((n_ex * ys,)),
                dma((n_ex * ys,)),
                dma((n_ex * n_tp,)),
            ],
            compiler_params=pltpu.CompilerParams(
                collective_id=0, has_side_effects=True, vmem_limit_bytes=40 * 1024 * 1024),
            cost_estimate=pl.CostEstimate(
                flops=2 * rows * width * n_ex * examples * tokens,
                bytes_accessed=12 * 1024 * 1024, transcendentals=0),
        )(
            pltpu.with_memory_space_constraint(flat, pltpu.HBM),
            pltpu.with_memory_space_constraint(out_grads, pltpu.HBM),
        )

    return jax.shard_map(
        body,
        mesh=mesh,
        in_specs=(P("ex", None, "tp"), P("ex", None, "tp")),
        out_specs=P("ex", "tp"),
        check_vma=False,
    )
```
